256 devices in a mesh: chan: 128 (over x_hi, y, z, core), tm: 2 (over x_lo).
Axes of the slice: x: 4 (x_hi: 2, x_lo: 2; x = x_hi * 2 + x_lo), y: 4, z: 8, core: 2. Of those that a mesh axis runs over, the one named last changes fastest.
Arguments:
- signal: bfloat16 [16384, 6144], P('chan', 'tm'), may hold values from -6 to 6
- fan_mask: int32 [128, 128], replicated, may hold values 0 or 1
Outputs:
- filtered: bfloat16 [16384, 6144], P('chan', 'tm')
The draws below stay inside these ranges and needn't reach their ends.
All inputs are finite; a program needn't handle non-finite values.
Results may differ from the reference program's by a relative error of at most 0.0063.
Values may be sent and summed in bfloat16 or wider, within the bound.
A program may use at most 64 MiB of HBM per device.

```python
import math
import jax
import jax.numpy as jnp
from jax import lax

WINDOW = 4096
BAND = 512
BIN_TILE = 4
WAVE_TILE = 128
CHANNELS = 16384
HOP = 2048
SAMPLES = 6144
BIN_TILES = 128
WAVE_TILES = 128


def set_ends(array, rng, smallest, top_value):
    longest = array.shape.index(max(array.shape))
    spots = []
    for shift in (0, 1):
        where = [jax.random.randint(jax.random.fold_in(rng, axis), (), 0, length) for axis, length in enumerate(array.shape)]
        where[longest] = (where[longest] + shift) % array.shape[longest]
        spots.append(tuple(where))
    return array.at[spots[0]].set(smallest).at[spots[1]].set(top_value)


def level_of(rng, extent, pieces, smallest, largest):
    def one(dim, blocks):
        draws = jax.random.uniform(jax.random.fold_in(jax.random.fold_in(rng, 6), dim), (blocks,), jnp.float32, smallest / len(pieces), largest / len(pieces))
        return jnp.repeat(jnp.exp(draws), extent[dim] // blocks).reshape((-1,) + (1,) * (len(extent) - dim - 1))

    gain = one(*pieces[0])
    for cut in pieces[1:]:
        gain = gain * one(*cut)
    return gain


def noise(stream_key, dims, spread, reach, pieces=(), held_as=jnp.bfloat16):
    loudness = level_of(stream_key, dims, pieces, -0.22, 0.18) if pieces else 1.0
    values = jax.random.normal(stream_key, dims, jnp.float32) * spread * loudness
    return jnp.minimum(jnp.maximum(values, -reach), reach).astype(held_as)


def setup_inputs(seed: int = 0) -> dict:
    streams_of = jax.random.split(jax.random.key(seed), 3)
    return {
        "signal": noise(streams_of[0], (CHANNELS, SAMPLES), 1.0, 6.0, ((0, 128), (1, 2))),
        "fan_mask": set_ends((jax.random.randint(streams_of[1], (BIN_TILES, WAVE_TILES), 0, 2) < 1).astype(jnp.int32), jax.random.fold_in(streams_of[1], 1), 0, 1),
    }


def time_tables():
    positions = jnp.arange(WINDOW, dtype=jnp.int32)
    bin_index = jnp.arange(BAND, dtype=jnp.int32)
    product = (positions[:, None] * bin_index[None, :]) % WINDOW
    phase_angle = (2.0 * math.pi / WINDOW) * product.astype(jnp.float32)
    forward = jnp.concatenate([jnp.cos(phase_angle), -jnp.sin(phase_angle)], axis=1).astype(jnp.bfloat16)
    weight = jnp.where(bin_index == 0, 1.0, 2.0).astype(jnp.float32)
    inverse = jnp.concatenate([weight[:, None] * jnp.cos(phase_angle).T, -weight[:, None] * jnp.sin(phase_angle).T], axis=0).astype(jnp.bfloat16)
    taper = 0.5 - 0.5 * jnp.cos((2.0 * math.pi / WINDOW) * positions.astype(jnp.float32))
    return forward, inverse, taper


def reference(signal, fan_mask):
    forward, inverse, taper = time_tables()
    row_block = math.gcd(CHANNELS, 2048)
    block_count = CHANNELS // row_block
    mask_full = jnp.repeat(jnp.repeat(fan_mask, BIN_TILE, axis=0), WAVE_TILE, axis=1).astype(jnp.float32).T

    def transform(rows):
        tapered = (rows.astype(jnp.float32) * taper).astype(jnp.bfloat16)
        return jnp.dot(tapered, forward, preferred_element_type=jnp.float32)

    def synthesize(rows):
        return jnp.dot(rows, inverse, preferred_element_type=jnp.float32) / WINDOW

    frames = []
    for window_number in range(2):
        offset_start = window_number * HOP
        segment = signal[:, offset_start:offset_start + WINDOW].reshape(block_count, row_block, WINDOW)
        spectrum = lax.map(transform, segment).reshape(CHANNELS, 2 * BAND)
        values = spectrum[:, :BAND] + 1j * spectrum[:, BAND:]
        wave = jnp.fft.fft(values, axis=0) * mask_full
        back = jnp.fft.ifft(wave, axis=0)
        parts = jnp.concatenate([jnp.real(back), jnp.imag(back)], axis=1).astype(jnp.bfloat16)
        frame = lax.map(synthesize, parts.reshape(block_count, row_block, 2 * BAND)).reshape(CHANNELS, WINDOW)
        frames.append(frame)
    first, second = frames
    joined = jnp.concatenate([first[:, :HOP], first[:, HOP:] + second[:, :HOP], second[:, HOP:]], axis=1)
    return joined.astype(jnp.bfloat16)
```

```python
import functools
import math

import jax
import jax.numpy as jnp
import ml_dtypes
import numpy as np
from jax import lax
from jax.experimental import pallas as pl
from jax.experimental.pallas import tpu as pltpu
from jax.sharding import PartitionSpec as P

WINDOW = 4096
BAND = 512
QUARTER = WINDOW // 4
LINES = 128
BINS = 4
ROWS = 2 * BINS
MESH = pl.DeviceIdType.MESH
F32 = jnp.float32
BF16 = jnp.bfloat16


def high_low(table):
    high = table.astype(ml_dtypes.bfloat16)
    low = (table - high.astype(np.float64)).astype(ml_dtypes.bfloat16)
    return high, low


@functools.cache
def tables():
    positions = np.arange(WINDOW)
    bins = np.arange(BAND)
    angle = 2.0 * math.pi / WINDOW * (positions[:, None] * bins[None, :] % WINDOW)
    cosine, sine = np.cos(angle), np.sin(angle)
    forward = np.stack([cosine, -sine], axis=1).reshape(WINDOW, 2, LINES, BINS)
    forward = forward.transpose(0, 2, 1, 3).reshape(4, QUARTER, 2 * BAND)
    weight = np.where(bins == 0, 1.0, 2.0)
    inverse = np.stack([weight * cosine, -weight * sine], axis=1).reshape(WINDOW, 2, LINES, BINS)
    inverse = inverse.transpose(2, 1, 3, 0).reshape(2 * BAND, 4, QUARTER).transpose(1, 0, 2)
    taper = (0.5 - 0.5 * np.cos(2.0 * math.pi / WINDOW * positions)).reshape(1, WINDOW)
    lines = np.arange(LINES)
    angle = 2.0 * math.pi / LINES * (lines[:, None] * lines[None, :] % LINES)
    cosine, sine = np.cos(angle), np.sin(angle)
    analysis = np.block([[cosine, sine], [-sine, cosine]])
    synthesis = np.block([[cosine, -sine], [sine, cosine]]) / LINES
    turns = np.stack(high_low(analysis) + high_low(synthesis))
    angle = 2.0 * math.pi / LINES**2 * (lines[:, None] * lines[None, :])
    fine = np.stack([np.cos(angle), np.sin(angle), cosine, sine]).astype(np.float32)
    return (
        forward.astype(ml_dtypes.bfloat16),
        inverse.astype(ml_dtypes.bfloat16),
        taper.astype(np.float32),
        turns,
        fine,
    )


def hops(step):
    core, z, y, x = step
    return min(z, 8 - z) + min(y, 4 - y) + 2 * x + 0.25 * core


def kernel(
    signal, mask, forward, inverse, taper, turns, fine, out,
    sig, mask_v, fwd, inv, taper_v, turns_v, fine_v, near, acc, send1, got1, send2, got2,
    lines_v, back_v, leaving, received,
    local, table_sem, link_send, link_recv,
):
    me, tm = lax.axis_index("chan"), lax.axis_index("tm")
    rem, div = lax.rem, lax.div
    core, z, y, x = rem(me, 2), rem(div(me, 2), 8), rem(div(me, 16), 4), div(me, 64)
    steps = [(c, k, j, i) for i in range(2) for j in range(4) for k in range(8) for c in range(2)]
    steps = sorted(steps[1:], key=hops, reverse=True)

    def device(step):
        c, k, j, i = step
        return ((rem(x + i, 2) * 4 + rem(y + j, 4)) * 8 + rem(z + k, 8)) * 2 + rem(core + c, 2)

    barrier = pltpu.get_barrier_semaphore()
    pl.semaphore_signal(barrier, 1, device_id={"tm": 1 - tm}, device_id_type=MESH)
    for step in steps:
        pl.semaphore_signal(barrier, 1, device_id={"chan": device(step)}, device_id_type=MESH)

    own = [tm + i for i in range(3)]
    other = 3 * (1 - tm)
    small = [(signal, sig), (taper, taper_v), (mask, mask_v), (fine, fine_v), (turns, turns_v)]
    small = [pltpu.make_async_copy(a, b, local.at[i]) for i, (a, b) in enumerate(small)]
    order = own + [other]
    fwd_copies = [pltpu.make_async_copy(forward.at[q], fwd.at[q], table_sem.at[i]) for i, q in enumerate(order)]
    inv_copies = [pltpu.make_async_copy(inverse.at[q], inv.at[q], table_sem.at[4 + q]) for q in range(4)]
    for copy in small + fwd_copies + inv_copies:
        copy.start()

    small[0].wait()
    pl.semaphore_wait(barrier, LINES)
    edge = pl.multiple_of((1 - tm) * 2 * QUARTER, QUARTER)
    swap = pltpu.make_async_remote_copy(
        sig.at[:, pl.ds(edge, QUARTER)], near, link_send.at[0], link_recv.at[0],
        device_id={"tm": 1 - tm}, device_id_type=MESH,
    )
    swap.start()

    for copy in small[1:]:
        copy.wait()
    passes = mask_v[pl.ds(me, 1), :].astype(F32) * (1.0 / LINES)
    cosine, sine = fine_v[2], fine_v[3]
    highest = lax.Precision.HIGHEST
    left = jnp.concatenate([cosine * passes, sine * passes], axis=1)
    right = jnp.concatenate(
        [jnp.concatenate([cosine, sine], axis=1), jnp.concatenate([sine, -cosine], axis=1)], axis=0
    )
    fan = jnp.dot(left, right, precision=highest, preferred_element_type=F32)
    fan = jnp.concatenate(
        [fan, jnp.concatenate([-fan[:, LINES:], fan[:, :LINES]], axis=1)], axis=0
    )
    fan_high = fan.astype(BF16)
    fan_low = (fan - fan_high.astype(F32)).astype(BF16)

    def part(samples, quarter):
        weights = taper_v[:, pl.ds(pl.multiple_of(quarter * QUARTER, QUARTER), QUARTER)]
        tapered = (samples.astype(F32) * weights).astype(BF16)
        return jnp.dot(tapered, fwd[quarter], preferred_element_type=F32)

    for i in range(3):
        fwd_copies[i].wait()
        term = part(sig[:, i * QUARTER : (i + 1) * QUARTER], own[i])
        if i == 0:
            acc[...] = term
        else:
            acc[...] += term
    fwd_copies[3].wait()
    swap.wait_recv()
    spectrum = acc[...] + part(near[...], other)
    send1[...] = spectrum.T.reshape(LINES, ROWS, LINES).astype(BF16)

    def exchange(source, target, slot):
        for step in steps:
            d = device(step)
            pltpu.make_async_remote_copy(
                source.at[d], target.at[me], link_send.at[slot], link_recv.at[slot],
                device_id={"chan": d}, device_id_type=MESH,
            ).start()
        target[me] = source[me]
        rest = pl.ds(0, LINES - 1)
        return pltpu.make_async_remote_copy(
            source.at[rest], target.at[rest], link_send.at[slot], link_recv.at[slot],
            device_id={"chan": device(steps[0])}, device_id_type=MESH,
        )

    first = exchange(send1, got1, 1)
    first.wait_recv()
    lines_v[...] = got1[...].astype(F32).reshape(ROWS * LINES, LINES)
    picked = [lines_v[pl.ds(r, LINES, stride=ROWS), :].astype(BF16) for r in range(ROWS)]
    stacked = jnp.concatenate(
        [jnp.concatenate(picked[:BINS], axis=1), jnp.concatenate(picked[BINS:], axis=1)], axis=0
    )
    wave = jnp.dot(turns_v[0], stacked, preferred_element_type=F32)
    wave += jnp.dot(turns_v[1], stacked, preferred_element_type=F32)
    twist_cos, twist_sin = fine_v[0], fine_v[1]
    turned = []
    for j in range(BINS):
        re = wave[:LINES, j * LINES : (j + 1) * LINES]
        im = wave[LINES:, j * LINES : (j + 1) * LINES]
        turned.append(
            jnp.concatenate(
                [re * twist_cos + im * twist_sin, im * twist_cos - re * twist_sin], axis=1
            )
        )
    turned = jnp.concatenate(turned, axis=0)
    high = turned.astype(BF16)
    low = (turned - high.astype(F32)).astype(BF16)
    masked = jnp.dot(high, fan_high, preferred_element_type=F32)
    masked += jnp.dot(low, fan_high, preferred_element_type=F32)
    masked += jnp.dot(high, fan_low, preferred_element_type=F32)
    real, imag = [], []
    for j in range(BINS):
        re = masked[j * LINES : (j + 1) * LINES, :LINES]
        im = masked[j * LINES : (j + 1) * LINES, LINES:]
        real.append(re * twist_cos - im * twist_sin)
        imag.append(im * twist_cos + re * twist_sin)
    straight = jnp.concatenate(
        [jnp.concatenate(real, axis=1), jnp.concatenate(imag, axis=1)], axis=0
    )
    high = straight.astype(BF16)
    low = (straight - high.astype(F32)).astype(BF16)
    back = jnp.dot(turns_v[2], high, preferred_element_type=F32)
    back += jnp.dot(turns_v[2], low, preferred_element_type=F32)
    back += jnp.dot(turns_v[3], high, preferred_element_type=F32)
    for r in range(ROWS):
        top, column = r // BINS * LINES, r % BINS * LINES
        lines_v[pl.ds(r, LINES, stride=ROWS), :] = back[top : top + LINES, column : column + LINES]
    send2[...] = lines_v[...].reshape(LINES, ROWS, LINES).astype(BF16)
    second = exchange(send2, got2, 2)
    for copy in inv_copies:
        copy.wait()
    second.wait_recv()
    back_v[...] = got2[...].astype(F32).reshape(ROWS * LINES, LINES).T.astype(BF16)

    def frame(quarter):
        return jnp.dot(back_v[...], inv[quarter], preferred_element_type=F32) * (1.0 / WINDOW)

    leaving[...] = frame(other).astype(BF16)
    tail = pltpu.make_async_remote_copy(
        leaving, received, link_send.at[3], link_recv.at[3],
        device_id={"tm": 1 - tm}, device_id_type=MESH,
    )
    tail.start()
    outer = pl.multiple_of(2 * QUARTER * tm, QUARTER)
    shared = pl.multiple_of(2 * QUARTER * (1 - tm), QUARTER)
    out[:, pl.ds(outer, QUARTER)] = frame(3 * tm).astype(BF16)
    out[:, QUARTER : 2 * QUARTER] = frame(1 + tm).astype(BF16)
    acc[...] = frame(2 - tm)
    tail.wait_recv()
    out[:, pl.ds(shared, QUARTER)] = (acc[...] + received[...].astype(F32)).astype(BF16)
    swap.wait_send()
    first.wait_send()
    second.wait_send()
    tail.wait_send()


def on_device(signal, fan_mask):
    anywhere = pl.BlockSpec(memory_space=pl.ANY)
    block = (LINES, ROWS, LINES)
    dma = pltpu.SemaphoreType.DMA
    vmem = pltpu.VMEM
    return pl.pallas_call(
        kernel,
        out_shape=jax.ShapeDtypeStruct(signal.shape, BF16),
        in_specs=[anywhere] * 7,
        out_specs=pl.BlockSpec(memory_space=pltpu.VMEM),
        scratch_shapes=[
            vmem(signal.shape, BF16),
            vmem((LINES, LINES), jnp.int32),
            vmem((4, QUARTER, 2 * BAND), BF16),
            vmem((4, 2 * BAND, QUARTER), BF16),
            vmem((1, WINDOW), F32),
            vmem((4, 2 * LINES, 2 * LINES), BF16),
            vmem((4, LINES, LINES), F32),
            vmem((LINES, QUARTER), BF16),
            vmem((LINES, 2 * BAND), F32),
            vmem(block, BF16),
            vmem(block, BF16),
            vmem(block, BF16),
            vmem(block, BF16),
            vmem((ROWS * LINES, LINES), F32),
            vmem((LINES, 2 * BAND), BF16),
            vmem((LINES, QUARTER), BF16),
            vmem((LINES, QUARTER), BF16),
            dma((5,)),
            dma((8,)),
            dma((4,)),
            dma((4,)),
        ],
        compiler_params=pltpu.CompilerParams(
            collective_id=0, has_side_effects=True, vmem_limit_bytes=48 * 2**20
        ),
        cost_estimate=pl.CostEstimate(
            flops=5 * 10**9, bytes_accessed=20 * 10**6, transcendentals=0
        ),
    )(signal, fan_mask, *tables())


def solution(mesh):
    return jax.shard_map(
        on_device,
        mesh=mesh,
        in_specs=(P("chan", "tm"), P()),
        out_specs=P("chan", "tm"),
        check_vma=False,
    )
```

```python
import functools
import math

import jax
import jax.numpy as jnp
import ml_dtypes
import numpy as np
from jax import lax
from jax.experimental import pallas as pl
from jax.experimental.pallas import tpu as pltpu
from jax.sharding import PartitionSpec as P

WINDOW = 4096
BAND = 512
QUARTER = WINDOW // 4
LINES = 128
BINS = 4
ROWS = 2 * BINS
MESH = pl.DeviceIdType.MESH
F32 = jnp.float32
BF16 = jnp.bfloat16


def high_low(table):
    high = table.astype(ml_dtypes.bfloat16)
    low = (table - high.astype(np.float64)).astype(ml_dtypes.bfloat16)
    return high, low


@functools.cache
def tables():
    positions = np.arange(WINDOW)
    bins = np.arange(BAND)
    angle = 2.0 * math.pi / WINDOW * (positions[:, None] * bins[None, :] % WINDOW)
    cosine, sine = np.cos(angle), np.sin(angle)
    places = np.arange(LINES).reshape(2, 4, 8, 2).transpose(2, 0, 1, 3).reshape(LINES)
    forward = np.stack([cosine, -sine], axis=1).reshape(WINDOW, 2, LINES, BINS)[:, :, places]
    forward = forward.transpose(0, 2, 1, 3).reshape(4, QUARTER, 2 * BAND)
    weight = np.where(bins == 0, 1.0, 2.0)
    inverse = np.stack([weight * cosine, -weight * sine], axis=1)
    inverse = inverse.reshape(WINDOW, 2, LINES, BINS)[:, :, places]
    inverse = inverse.transpose(2, 1, 3, 0).reshape(2 * BAND, 4, QUARTER).transpose(1, 0, 2)
    taper = (0.5 - 0.5 * np.cos(2.0 * math.pi / WINDOW * positions)).reshape(1, WINDOW)
    lines = np.arange(LINES)
    angle = 2.0 * math.pi / LINES * (lines[:, None] * lines[None, :] % LINES)
    cosine, sine = np.cos(angle), np.sin(angle)
    analysis = np.block([[cosine, sine], [-sine, cosine]])[:, np.r_[places, LINES + places]]
    synthesis = np.block([[cosine, -sine], [sine, cosine]])[np.r_[places, LINES + places]] / LINES
    turns = np.stack(high_low(analysis) + high_low(synthesis))
    angle = 2.0 * math.pi / LINES**2 * (lines[:, None] * lines[None, :])
    fine = np.stack([np.cos(angle), np.sin(angle), cosine, sine]).astype(np.float32)
    return (
        forward.astype(ml_dtypes.bfloat16),
        inverse.astype(ml_dtypes.bfloat16),
        taper.astype(np.float32),
        turns,
        fine,
    )


def hops(step):
    x, y, core = step
    return 2 * x + min(y, 4 - y) + 0.25 * core


LAYERS = 8
AROUND = LINES // LAYERS
Z_STEPS = (4, 3, 5, 2, 6, 1, 7, 0)
PLANE_STEPS = sorted(((i, j, c) for i in range(2) for j in range(4) for c in range(2)), key=hops, reverse=True)


def kernel(
    signal, mask, forward, inverse, taper, turns, fine, out,
    sig, mask_v, fwd, inv, taper_v, turns_v, fine_v, own_part, other_part, arrived_part,
    send1, got1, send2, got2, passed, lines_v, back_v, other_v,
    local, table_sem, swap_send, swap_recv, send_sem, recv1, recv2, pass_send, pass_recv,
):
    me, tm = lax.axis_index("chan"), lax.axis_index("tm")
    rem, div = lax.rem, lax.div
    core, z, y, x = rem(me, 2), rem(div(me, 2), 8), rem(div(me, 16), 4), div(me, 64)
    layers = [rem(z + k, LAYERS) for k in Z_STEPS]
    plane = [(rem(x + i, 2), rem(y + j, 4), rem(core + c, 2)) for i, j, c in PLANE_STEPS]
    here = z * AROUND + (x * 4 + y) * 2 + core
    partner = {"tm": 1 - tm}

    def peers(layer, first):
        for i, j, c in plane[: AROUND - first]:
            yield layer * AROUND + (i * 4 + j) * 2 + c, ((i * 4 + j) * 8 + layer) * 2 + c

    everyone = [(k, peers(layer, Z_STEPS[k] == 0)) for k, layer in enumerate(layers)]
    everyone = [list(p) for _, p in everyone]

    barrier = pltpu.get_barrier_semaphore()
    pl.semaphore_signal(barrier, 1, device_id=partner, device_id_type=MESH)
    for group in everyone:
        for _, d in group:
            pl.semaphore_signal(barrier, 1, device_id={"chan": d}, device_id_type=MESH)

    small = [(signal, sig), (taper, taper_v), (mask, mask_v), (fine, fine_v), (turns, turns_v)]
    small = [pltpu.make_async_copy(a, b, local.at[i]) for i, (a, b) in enumerate(small)]
    edge = 3 * tm
    quarters = [edge, 1, 2]
    fwd_copies = [pltpu.make_async_copy(forward.at[q], fwd.at[i], table_sem.at[i]) for i, q in enumerate(quarters)]
    inv_copies = [pltpu.make_async_copy(inverse.at[q], inv.at[i], table_sem.at[3 + i]) for i, q in enumerate(quarters)]
    for copy in small + fwd_copies + inv_copies:
        copy.start()

    outer = pl.multiple_of(2 * QUARTER * tm, QUARTER)
    shared = pl.multiple_of(2 * QUARTER * (1 - tm), QUARTER)

    def tapered(offset, quarter):
        weights = taper_v[:, pl.ds(pl.multiple_of(quarter * QUARTER, QUARTER), QUARTER)]
        return (sig[:, pl.ds(offset, QUARTER)].astype(F32) * weights).astype(BF16)

    small[0].wait()
    small[1].wait()
    both = jnp.concatenate([tapered(shared, edge), tapered(outer, edge)], axis=0)
    fwd_copies[0].wait()
    both = jnp.dot(both, fwd[0], preferred_element_type=F32)
    other_part[...] = both[:LINES].T.reshape(LAYERS, LINES, LINES).astype(BF16)
    pl.semaphore_wait(barrier, LINES)
    swaps = []
    for k, layer in enumerate(layers):
        swaps.append(
            pltpu.make_async_remote_copy(
                other_part.at[layer], arrived_part.at[layer], swap_send.at[k], swap_recv.at[k],
                device_id=partner, device_id_type=MESH,
            )
        )
        swaps[-1].start()
    middle = [pl.multiple_of(QUARTER * (1 - tm), QUARTER), pl.multiple_of(QUARTER * (2 - tm), QUARTER)]
    total = both[LINES:]
    for i in range(2):
        fwd_copies[1 + i].wait()
        total += jnp.dot(tapered(middle[i], 1 + i), fwd[1 + i], preferred_element_type=F32)
    own_part[...] = total.T.reshape(LAYERS, LINES, LINES)

    def start(source, target, place, d, send, recv):
        pltpu.make_async_remote_copy(
            source.at[place], target.at[here], send, recv, device_id={"chan": d}, device_id_type=MESH
        ).start()

    for k, layer in enumerate(layers):
        swaps[k].wait_recv()
        lines = own_part[layer] + arrived_part[layer].astype(F32)
        send1[pl.ds(layer * AROUND, AROUND)] = lines.reshape(AROUND, ROWS, LINES).astype(BF16)
        for place, d in everyone[k]:
            start(send1, got1, place, d, send_sem.at[0], recv1)
    got1[here] = send1[here]

    for copy in small[2:]:
        copy.wait()
    passes = mask_v[pl.ds(me, 1), :].astype(F32) * (1.0 / LINES)
    cosine, sine = fine_v[2], fine_v[3]
    left = jnp.concatenate([cosine * passes, sine * passes], axis=1)
    right = jnp.concatenate(
        [jnp.concatenate([cosine, sine], axis=1), jnp.concatenate([sine, -cosine], axis=1)], axis=0
    )
    fan = jnp.dot(left, right, precision=lax.Precision.HIGHEST, preferred_element_type=F32)
    fan = jnp.concatenate(
        [fan, jnp.concatenate([-fan[:, LINES:], fan[:, :LINES]], axis=1)], axis=0
    )
    fan_high = fan.astype(BF16)
    fan_low = (fan - fan_high.astype(F32)).astype(BF16)

    def whole(source, target, send, recv):
        rest = pl.ds(0, LINES - 1)
        return pltpu.make_async_remote_copy(
            source.at[rest], target.at[rest], send, recv,
            device_id={"chan": everyone[0][0][1]}, device_id_type=MESH,
        )

    first = whole(send1, got1, send_sem.at[0], recv1)
    first.wait_recv()
    lines_v[...] = got1[...].astype(F32).reshape(ROWS * LINES, LINES)
    picked = [lines_v[pl.ds(r, LINES, stride=ROWS), :].astype(BF16) for r in range(ROWS)]
    stacked = jnp.concatenate(
        [jnp.concatenate(picked[:BINS], axis=1), jnp.concatenate(picked[BINS:], axis=1)], axis=0
    )
    wave = jnp.dot(turns_v[0], stacked, preferred_element_type=F32)
    wave += jnp.dot(turns_v[1], stacked, preferred_element_type=F32)
    twist_cos, twist_sin = fine_v[0], fine_v[1]
    turned = []
    for j in range(BINS):
        re = wave[:LINES, j * LINES : (j + 1) * LINES]
        im = wave[LINES:, j * LINES : (j + 1) * LINES]
        turned.append(
            jnp.concatenate(
                [re * twist_cos + im * twist_sin, im * twist_cos - re * twist_sin], axis=1
            )
        )
    turned = jnp.concatenate(turned, axis=0)
    high = turned.astype(BF16)
    low = (turned - high.astype(F32)).astype(BF16)
    masked = jnp.dot(high, fan_high, preferred_element_type=F32)
    masked += jnp.dot(low, fan_high, preferred_element_type=F32)
    masked += jnp.dot(high, fan_low, preferred_element_type=F32)
    real, imag = [], []
    for j in range(BINS):
        re = masked[j * LINES : (j + 1) * LINES, :LINES]
        im = masked[j * LINES : (j + 1) * LINES, LINES:]
        real.append(re * twist_cos - im * twist_sin)
        imag.append(im * twist_cos + re * twist_sin)
    straight = jnp.concatenate(
        [jnp.concatenate(real, axis=1), jnp.concatenate(imag, axis=1)], axis=0
    )
    high = straight.astype(BF16)
    low = (straight - high.astype(F32)).astype(BF16)
    back = jnp.dot(turns_v[2], high, preferred_element_type=F32)
    back += jnp.dot(turns_v[2], low, preferred_element_type=F32)
    back += jnp.dot(turns_v[3], high, preferred_element_type=F32)
    for r in range(ROWS):
        top, column = r // BINS * LINES, r % BINS * LINES
        lines_v[pl.ds(r, LINES, stride=ROWS), :] = back[top : top + LINES, column : column + LINES]
    send2[...] = lines_v[...].reshape(LINES, ROWS, LINES).astype(BF16)
    for group in everyone:
        for place, d in group:
            start(send2, got2, place, d, send_sem.at[1], recv2.at[z])
    got2[here] = send2[here]

    def turn(source, target, layer):
        block = source[pl.ds(layer * AROUND, AROUND)].astype(F32).reshape(LINES, LINES)
        target[:, pl.ds(pl.multiple_of(layer * LINES, LINES), LINES)] = block.T.astype(BF16)

    passing = []
    for k, layer in enumerate(layers):
        count = pl.ds(0, len(everyone[k]))
        pltpu.make_async_remote_copy(
            send2.at[count], got2.at[count], send_sem.at[1], recv2.at[layer],
            device_id=partner, device_id_type=MESH,
        ).wait_recv()
        block = pl.ds(layer * AROUND, AROUND)
        passing.append(
            pltpu.make_async_remote_copy(
                got2.at[block], passed.at[block], pass_send.at[k], pass_recv.at[k],
                device_id=partner, device_id_type=MESH,
            )
        )
        passing[-1].start()
        turn(got2, back_v, layer)

    def frame(values, i):
        return jnp.dot(values, inv[i], preferred_element_type=F32) * (1.0 / WINDOW)

    for copy in inv_copies:
        copy.wait()
    out[:, pl.ds(outer, QUARTER)] = frame(back_v[...], 0).astype(BF16)
    centre = 1 + tm
    out[:, QUARTER : 2 * QUARTER] = frame(back_v[...], centre).astype(BF16)
    overlap = frame(back_v[...], 2 - tm)
    for k, layer in enumerate(layers):
        passing[k].wait_recv()
        turn(passed, other_v, layer)
    out[:, pl.ds(shared, QUARTER)] = (overlap + frame(other_v[...], 0)).astype(BF16)
    for copy in swaps + passing:
        copy.wait_send()
    first.wait_send()
    whole(send2, got2, send_sem.at[1], recv1).wait_send()


def on_device(signal, fan_mask):
    far = pl.BlockSpec(memory_space=pltpu.HBM)
    block = (LINES, ROWS, LINES)
    dma = pltpu.SemaphoreType.DMA
    vmem = pltpu.VMEM
    return pl.pallas_call(
        kernel,
        out_shape=jax.ShapeDtypeStruct(signal.shape, BF16),
        in_specs=[far] * 7,
        out_specs=pl.BlockSpec(memory_space=pltpu.VMEM),
        scratch_shapes=[
            vmem(signal.shape, BF16),
            vmem((LINES, LINES), jnp.int32),
            vmem((3, QUARTER, 2 * BAND), BF16),
            vmem((3, 2 * BAND, QUARTER), BF16),
            vmem((1, WINDOW), F32),
            vmem((4, 2 * LINES, 2 * LINES), BF16),
            vmem((4, LINES, LINES), F32),
            vmem((LAYERS, LINES, LINES), F32),
            vmem((LAYERS, LINES, LINES), BF16),
            vmem((LAYERS, LINES, LINES), BF16),
            vmem(block, BF16),
            vmem(block, BF16),
            vmem(block, BF16),
            vmem(block, BF16),
            vmem(block, BF16),
            vmem((ROWS * LINES, LINES), F32),
            vmem((LINES, 2 * BAND), BF16),
            vmem((LINES, 2 * BAND), BF16),
            dma((5,)),
            dma((6,)),
            dma((LAYERS,)),
            dma((LAYERS,)),
            dma((2,)),
            dma(()),
            dma((LAYERS,)),
            dma((LAYERS,)),
            dma((LAYERS,)),
        ],
        compiler_params=pltpu.CompilerParams(
            collective_id=0, has_side_effects=True, vmem_limit_bytes=56 * 2**20
        ),
        cost_estimate=pl.CostEstimate(
            flops=5 * 10**9, bytes_accessed=20 * 10**6, transcendentals=0
        ),
    )(signal, fan_mask, *tables())


def solution(mesh):
    return jax.shard_map(
        on_device,
        mesh=mesh,
        in_specs=(P("chan", "tm"), P()),
        out_specs=P("chan", "tm"),
        check_vma=False,
    )
```

```python
import functools
import math

import jax
import jax.numpy as jnp
import ml_dtypes
import numpy as np
from jax import lax
from jax.experimental import pallas as pl
from jax.experimental.pallas import tpu as pltpu
from jax.sharding import PartitionSpec as P

WINDOW = 4096
BAND = 512
QUARTER = WINDOW // 4
LINES = 128
BINS = 4
ROWS = 2 * BINS
MESH = pl.DeviceIdType.MESH
F32 = jnp.float32
BF16 = jnp.bfloat16


def high_low(table):
    high = table.astype(ml_dtypes.bfloat16)
    low = (table - high.astype(np.float64)).astype(ml_dtypes.bfloat16)
    return high, low


@functools.cache
def tables():
    positions = np.arange(WINDOW)
    bins = np.arange(BAND)
    angle = 2.0 * math.pi / WINDOW * (positions[:, None] * bins[None, :] % WINDOW)
    cosine, sine = np.cos(angle), np.sin(angle)
    grid = np.arange(LINES).reshape(2, 4, LAYERS, 2)
    owners = grid.transpose(0, 2, 1, 3).reshape(LINES)
    sources = grid.transpose(2, 1, 3, 0).reshape(LINES)
    forward = np.stack([cosine, -sine], axis=1).reshape(WINDOW, 2, LINES, BINS)[:, :, owners]
    forward = forward.transpose(0, 2, 1, 3).reshape(4, QUARTER, 2 * BAND)
    weight = np.where(bins == 0, 1.0, 2.0)
    inverse = np.stack([weight * cosine, -weight * sine], axis=1)
    inverse = inverse.reshape(WINDOW, 2, LINES, BINS)[:, :, owners]
    inverse = inverse.transpose(2, 1, 3, 0).reshape(2 * BAND, 4, QUARTER).transpose(1, 0, 2)
    taper = (0.5 - 0.5 * np.cos(2.0 * math.pi / WINDOW * positions)).reshape(1, WINDOW)
    lines = np.arange(LINES)
    angle = 2.0 * math.pi / LINES * (lines[:, None] * lines[None, :] % LINES)
    cosine, sine = np.cos(angle), np.sin(angle)
    order = np.r_[sources, LINES + sources]
    analysis = np.block([[cosine, sine], [-sine, cosine]])[:, order]
    synthesis = np.block([[cosine, -sine], [sine, cosine]])[order] / LINES
    turns = np.stack(high_low(analysis) + high_low(synthesis))
    angle = 2.0 * math.pi / LINES**2 * (lines[:, None] * lines[None, :])
    fine = np.stack([np.cos(angle), np.sin(angle), cosine, sine]).astype(np.float32)
    return (
        forward.astype(ml_dtypes.bfloat16),
        inverse.astype(ml_dtypes.bfloat16),
        taper.astype(np.float32),
        turns,
        fine,
    )


LAYERS = 8
AROUND = 8
PLANE = LAYERS * AROUND
Z_STEPS = (4, 3, 5, 2, 6, 1, 7, 0)
Y_STEPS = ((2, 1), (2, 0), (1, 1), (3, 1), (1, 0), (3, 0), (0, 1), (0, 0))


def kernel(
    signal, mask, forward, inverse, taper, turns, fine, out,
    sig, mask_v, fwd, inv, taper_v, turns_v, fine_v, own_part, own_send, other_part, summands,
    send1, got1, send2, got2, passed, lines_v, back_v, other_v,
    local, table_sem, sum_send, sum_recv, send_sem, recv1, recv2, pass_send, pass_recv,
):
    me, tm = lax.axis_index("chan"), lax.axis_index("tm")
    rem, div = lax.rem, lax.div
    core, z, y, x = rem(me, 2), rem(div(me, 2), 8), rem(div(me, 16), 4), div(me, 64)
    layers = [rem(z + k, LAYERS) for k in Z_STEPS]
    spots = [(rem(y + j, 4), rem(core + c, 2)) for j, c in Y_STEPS]
    here = (z * 4 + y) * 2 + core
    across = me + PLANE * (1 - 2 * x)
    partner, far, diagonal = {"tm": 1 - tm}, {"chan": across}, {"chan": across, "tm": 1 - tm}

    everyone = []
    for k, layer in enumerate(layers):
        group = spots if Z_STEPS[k] else spots[:-1]
        everyone.append([((layer * 4 + j) * 2 + c, ((x * 4 + j) * 8 + layer) * 2 + c) for j, c in group])

    barrier = pltpu.get_barrier_semaphore()
    for peer in (far, diagonal, partner):
        pl.semaphore_signal(barrier, 1, device_id=peer, device_id_type=MESH)
    for group in everyone:
        for _, d in group:
            pl.semaphore_signal(barrier, 1, device_id={"chan": d}, device_id_type=MESH)

    small = [(signal, sig), (taper, taper_v), (mask, mask_v), (fine, fine_v), (turns, turns_v)]
    small = [pltpu.make_async_copy(a, b, local.at[i]) for i, (a, b) in enumerate(small)]
    edge = 3 * tm
    quarters = [edge, 1, 2]
    fwd_copies = [pltpu.make_async_copy(forward.at[q], fwd.at[i], table_sem.at[i]) for i, q in enumerate(quarters)]
    inv_copies = [pltpu.make_async_copy(inverse.at[q], inv.at[i], table_sem.at[3 + i]) for i, q in enumerate(quarters)]
    for copy in small[:2] + fwd_copies + small[2:] + inv_copies:
        copy.start()

    outer = pl.multiple_of(2 * QUARTER * tm, QUARTER)
    shared = pl.multiple_of(2 * QUARTER * (1 - tm), QUARTER)

    def tapered(offset, quarter):
        weights = taper_v[:, pl.ds(pl.multiple_of(quarter * QUARTER, QUARTER), QUARTER)]
        return (sig[:, pl.ds(offset, QUARTER)].astype(F32) * weights).astype(BF16)

    shape = (2, LAYERS, AROUND * ROWS, LINES)
    small[0].wait()
    small[1].wait()
    both = jnp.concatenate([tapered(shared, edge), tapered(outer, edge)], axis=0)
    fwd_copies[0].wait()
    both = jnp.dot(both, fwd[0], preferred_element_type=F32)
    other_part[...] = both[:LINES].T.reshape(shape).astype(BF16)
    middle = [pl.multiple_of(QUARTER * (1 - tm), QUARTER), pl.multiple_of(QUARTER * (2 - tm), QUARTER)]
    total = both[LINES:]
    for i in range(2):
        fwd_copies[1 + i].wait()
        total += jnp.dot(tapered(middle[i], 1 + i), fwd[1 + i], preferred_element_type=F32)
    own_part[...] = total.T.reshape(shape)
    own_send[...] = own_part[1 - x].astype(BF16)

    pl.semaphore_wait(barrier, PLANE + 2)
    sums = []
    for k, layer in enumerate(layers):
        sources = (other_part.at[x, layer], own_send.at[layer], other_part.at[1 - x, layer])
        sums.append(
            [
                pltpu.make_async_remote_copy(
                    source, summands.at[i, layer], sum_send, sum_recv.at[i, k],
                    device_id=peer, device_id_type=MESH,
                )
                for i, (source, peer) in enumerate(zip(sources, (partner, far, diagonal)))
            ]
        )
        for i in (1, 2, 0):
            sums[k][i].start()

    for k, layer in enumerate(layers):
        for copy in sums[k]:
            copy.wait_recv()
        block = pl.ds(layer * AROUND, AROUND)
        mine = own_part[x, layer] + summands[0, layer].astype(F32)
        theirs = summands[1, layer].astype(F32) + summands[2, layer].astype(F32)
        send1[block, x] = mine.reshape(AROUND, ROWS, LINES).astype(BF16)
        send1[block, 1 - x] = theirs.reshape(AROUND, ROWS, LINES).astype(BF16)
        for place, d in everyone[k]:
            pltpu.make_async_remote_copy(
                send1.at[place], got1.at[here], send_sem.at[0], recv1,
                device_id={"chan": d}, device_id_type=MESH,
            ).start()
    got1[here] = send1[here]

    for copy in small[2:]:
        copy.wait()
    passes = mask_v[pl.ds(me, 1), :].astype(F32) * (1.0 / LINES)
    cosine, sine = fine_v[2], fine_v[3]
    left = jnp.concatenate([cosine * passes, sine * passes], axis=1)
    right = jnp.concatenate(
        [jnp.concatenate([cosine, sine], axis=1), jnp.concatenate([sine, -cosine], axis=1)], axis=0
    )
    fan = jnp.dot(left, right, precision=lax.Precision.HIGHEST, preferred_element_type=F32)
    fan = jnp.concatenate(
        [fan, jnp.concatenate([-fan[:, LINES:], fan[:, :LINES]], axis=1)], axis=0
    )
    fan_high = fan.astype(BF16)
    fan_low = (fan - fan_high.astype(F32)).astype(BF16)

    rest = pl.ds(0, PLANE - 1)
    first = pltpu.make_async_remote_copy(
        send1.at[rest], got1.at[rest], send_sem.at[0], recv1, device_id=partner, device_id_type=MESH
    )
    first.wait_recv()
    lines_v[...] = got1[...].astype(F32).reshape(ROWS * LINES, LINES)
    picked = [lines_v[pl.ds(r, LINES, stride=ROWS), :].astype(BF16) for r in range(ROWS)]
    stacked = jnp.concatenate(
        [jnp.concatenate(picked[:BINS], axis=1), jnp.concatenate(picked[BINS:], axis=1)], axis=0
    )
    wave = jnp.dot(turns_v[0], stacked, preferred_element_type=F32)
    wave += jnp.dot(turns_v[1], stacked, preferred_element_type=F32)
    twist_cos, twist_sin = fine_v[0], fine_v[1]
    turned = []
    for j in range(BINS):
        re = wave[:LINES, j * LINES : (j + 1) * LINES]
        im = wave[LINES:, j * LINES : (j + 1) * LINES]
        turned.append(
            jnp.concatenate(
                [re * twist_cos + im * twist_sin, im * twist_cos - re * twist_sin], axis=1
            )
        )
    turned = jnp.concatenate(turned, axis=0)
    high = turned.astype(BF16)
    low = (turned - high.astype(F32)).astype(BF16)
    masked = jnp.dot(high, fan_high, preferred_element_type=F32)
    masked += jnp.dot(low, fan_high, preferred_element_type=F32)
    masked += jnp.dot(high, fan_low, preferred_element_type=F32)
    real, imag = [], []
    for j in range(BINS):
        re = masked[j * LINES : (j + 1) * LINES, :LINES]
        im = masked[j * LINES : (j + 1) * LINES, LINES:]
        real.append(re * twist_cos - im * twist_sin)
        imag.append(im * twist_cos + re * twist_sin)
    straight = jnp.concatenate(
        [jnp.concatenate(real, axis=1), jnp.concatenate(imag, axis=1)], axis=0
    )
    high = straight.astype(BF16)
    low = (straight - high.astype(F32)).astype(BF16)
    back = jnp.dot(turns_v[2], high, preferred_element_type=F32)
    back += jnp.dot(turns_v[2], low, preferred_element_type=F32)
    back += jnp.dot(turns_v[3], high, preferred_element_type=F32)
    for r in range(ROWS):
        top, column = r // BINS * LINES, r % BINS * LINES
        lines_v[pl.ds(r, LINES, stride=ROWS), :] = back[top : top + LINES, column : column + LINES]
    send2[...] = lines_v[...].reshape(PLANE, 2, ROWS, LINES).astype(BF16)

    halves = (1 - x, x)
    for i, half in enumerate(halves):
        for group in everyone:
            for place, d in group:
                pltpu.make_async_remote_copy(
                    send2.at[place, half], got2.at[half, here], send_sem.at[1], recv2.at[i, z],
                    device_id={"chan": d}, device_id_type=MESH,
                ).start()
        got2[half, here] = send2[here, half]

    for i, half in enumerate(halves):
        for k, layer in enumerate(layers):
            count = got2.at[half, pl.ds(0, len(everyone[k]))]
            pltpu.make_async_remote_copy(
                count, count, send_sem.at[1], recv2.at[i, layer],
                device_id=partner, device_id_type=MESH,
            ).wait_recv()
            block = pl.ds(layer * AROUND, AROUND)
            for kind, peer in ((1, far), (2, diagonal)) if i == 0 else ((0, partner),):
                pltpu.make_async_remote_copy(
                    got2.at[half, block], passed.at[kind, block], pass_send, pass_recv.at[kind],
                    device_id=peer, device_id_type=MESH,
                ).start()

    def turn(block, target, half):
        lines = block.astype(F32).reshape(BAND, LINES).T
        target[:, pl.ds(pl.multiple_of(half * BAND, BAND), BAND)] = lines.astype(BF16)

    def arrived(kind):
        pltpu.make_async_remote_copy(
            passed.at[kind], passed.at[kind], pass_send, pass_recv.at[kind],
            device_id=partner, device_id_type=MESH,
        ).wait_recv()
        return passed[kind]

    def frame(values, i):
        return jnp.dot(values, inv[i], preferred_element_type=F32) * (1.0 / WINDOW)

    turn(got2[x], back_v, x)
    for copy in inv_copies:
        copy.wait()
    turn(arrived(1), back_v, 1 - x)
    out[:, pl.ds(outer, QUARTER)] = frame(back_v[...], 0).astype(BF16)
    centre = 1 + tm
    out[:, QUARTER : 2 * QUARTER] = frame(back_v[...], centre).astype(BF16)
    overlap = frame(back_v[...], 2 - tm)
    turn(arrived(2), other_v, 1 - x)
    turn(arrived(0), other_v, x)
    out[:, pl.ds(shared, QUARTER)] = (overlap + frame(other_v[...], 0)).astype(BF16)

    def sent(ref, sem):
        pltpu.make_async_remote_copy(
            ref, ref, sem, recv1, device_id=partner, device_id_type=MESH
        ).wait_send()

    sent(summands, sum_send)
    first.wait_send()
    sent(send2.at[rest], send_sem.at[1])
    sent(passed, pass_send)


def on_device(signal, fan_mask):
    far = pl.BlockSpec(memory_space=pltpu.HBM)
    block = (PLANE, 2, ROWS, LINES)
    spectra = (LAYERS, AROUND * ROWS, LINES)
    dma = pltpu.SemaphoreType.DMA
    vmem = pltpu.VMEM
    return pl.pallas_call(
        kernel,
        out_shape=jax.ShapeDtypeStruct(signal.shape, BF16),
        in_specs=[far] * 7,
        out_specs=pl.BlockSpec(memory_space=pltpu.VMEM),
        scratch_shapes=[
            vmem(signal.shape, BF16),
            vmem((LINES, LINES), jnp.int32),
            vmem((3, QUARTER, 2 * BAND), BF16),
            vmem((3, 2 * BAND, QUARTER), BF16),
            vmem((1, WINDOW), F32),
            vmem((4, 2 * LINES, 2 * LINES), BF16),
            vmem((4, LINES, LINES), F32),
            vmem((2, *spectra), F32),
            vmem(spectra, BF16),
            vmem((2, *spectra), BF16),
            vmem((3, *spectra), BF16),
            vmem(block, BF16),
            vmem(block, BF16),
            vmem(block, BF16),
            vmem((2, PLANE, ROWS, LINES), BF16),
            vmem((3, PLANE, ROWS, LINES), BF16),
            vmem((ROWS * LINES, LINES), F32),
            vmem((LINES, 2 * BAND), BF16),
            vmem((LINES, 2 * BAND), BF16),
            dma((5,)),
            dma((6,)),
            dma(()),
            dma((3, LAYERS)),
            dma((2,)),
            dma(()),
            dma((2, LAYERS)),
            dma(()),
            dma((3,)),
        ],
        compiler_params=pltpu.CompilerParams(
            collective_id=0, has_side_effects=True, vmem_limit_bytes=56 * 2**20
        ),
        cost_estimate=pl.CostEstimate(
            flops=5 * 10**9, bytes_accessed=20 * 10**6, transcendentals=0
        ),
    )(signal, fan_mask, *tables())


def solution(mesh):
    return jax.shard_map(
        on_device,
        mesh=mesh,
        in_specs=(P("chan", "tm"), P()),
        out_specs=P("chan", "tm"),
        check_vma=False,
    )
```

```python
import functools
import math

import jax
import jax.numpy as jnp
import ml_dtypes
import numpy as np
from jax import lax
from jax.experimental import pallas as pl
from jax.experimental.pallas import tpu as pltpu
from jax.sharding import PartitionSpec as P

WINDOW = 4096
BAND = 512
QUARTER = WINDOW // 4
LINES = 128
BINS = 4
PAIR = BINS // 2
ROWS = 2 * BINS
MESH = pl.DeviceIdType.MESH
F32 = jnp.float32
BF16 = jnp.bfloat16


def high_low(table):
    high = table.astype(ml_dtypes.bfloat16)
    low = (table - high.astype(np.float64)).astype(ml_dtypes.bfloat16)
    return high, low


@functools.cache
def tables():
    positions = np.arange(WINDOW)
    bins = np.arange(BAND)
    angle = 2.0 * math.pi / WINDOW * (positions[:, None] * bins[None, :] % WINDOW)
    cosine, sine = np.cos(angle), np.sin(angle)
    grid = np.arange(LINES).reshape(2, 4, LAYERS, 2)
    owners = grid.transpose(0, 2, 1, 3).reshape(LINES)
    places = [(WINDOW, 2, 2, PLANE, 2, PAIR), (0, 2, 4, 3, 1, 5)]
    forward = np.stack([cosine, -sine], axis=1).reshape(WINDOW, 2, LINES, BINS)[:, :, owners]
    forward = forward.reshape(places[0]).transpose(places[1]).reshape(4, QUARTER, 2 * BAND)
    weight = np.where(bins == 0, 1.0, 2.0)
    inverse = np.stack([weight * cosine, -weight * sine], axis=1)
    inverse = inverse.reshape(WINDOW, 2, LINES, BINS)[:, :, owners]
    inverse = inverse.reshape(places[0]).transpose(places[1]).reshape(4, QUARTER, 2 * BAND)
    inverse = inverse.transpose(0, 2, 1)
    taper = (0.5 - 0.5 * np.cos(2.0 * math.pi / WINDOW * positions)).reshape(1, WINDOW)
    lines = np.arange(LINES)
    angle = 2.0 * math.pi / LINES * (lines[:, None] * lines[None, :] % LINES)
    cosine, sine = np.cos(angle), np.sin(angle)
    order = np.r_[owners, LINES + owners]
    analysis = np.block([[cosine, sine], [-sine, cosine]])[:, order]
    synthesis = np.block([[cosine, -sine], [sine, cosine]])[order] / LINES
    turns = np.stack(high_low(analysis) + high_low(synthesis))
    angle = 2.0 * math.pi / LINES**2 * (lines[:, None] * lines[None, :])
    fine = np.stack([np.cos(angle), np.sin(angle), cosine, sine]).astype(np.float32)
    return (
        forward.astype(ml_dtypes.bfloat16),
        inverse.astype(ml_dtypes.bfloat16),
        taper.astype(np.float32),
        turns,
        fine,
    )


LAYERS = 8
AROUND = 8
PLANE = LAYERS * AROUND
GROUP = AROUND * 2 * PAIR
Z_STEPS = (4, 3, 5, 2, 6, 1, 7, 0)
AHEAD = 8
Y_STEPS = ((2, 1), (2, 0), (1, 1), (3, 1), (1, 0), (3, 0), (0, 1), (0, 0))


def regroup(first, second):
    upper = jnp.concatenate([first[:, :4], second[:, :4]], axis=1)
    return upper, jnp.concatenate([first[:, 4:], second[:, 4:]], axis=1)


def kernel(
    signal, mask, forward, inverse, taper, turns, fine, out,
    sig, mask_v, fwd, inv, taper_v, turns_v, fine_v, own_part, own_send, other_part, summands,
    send1, got1, send2, got2, kept, leaving, passed, lines_v, back_v, other_v,
    local, table_sem, sum_send, sum_recv, send_sem, recv1, recv2, pass_send, pass_recv,
):
    me, tm = lax.axis_index("chan"), lax.axis_index("tm")
    rem, div = lax.rem, lax.div
    core, z, y, x = rem(me, 2), rem(div(me, 2), 8), rem(div(me, 16), 4), div(me, 64)
    layers = [rem(z + k, LAYERS) for k in Z_STEPS]
    spots = [(rem(y + j, 4), rem(core + c, 2)) for j, c in Y_STEPS]
    here = (z * 4 + y) * 2 + core
    across = me + PLANE * (1 - 2 * x)
    partner, far, diagonal = {"tm": 1 - tm}, {"chan": across}, {"chan": across, "tm": 1 - tm}

    everyone = []
    for k, layer in enumerate(layers):
        group = spots if Z_STEPS[k] else spots[:-1]
        everyone.append([((layer * 4 + j) * 2 + c, ((x * 4 + j) * 8 + layer) * 2 + c) for j, c in group])

    barrier = pltpu.get_barrier_semaphore()
    for peer in (far, diagonal, partner):
        pl.semaphore_signal(barrier, 1, device_id=peer, device_id_type=MESH)
    for group in everyone:
        for _, d in group:
            pl.semaphore_signal(barrier, 1, device_id={"chan": d}, device_id_type=MESH)

    small = [(signal, sig), (taper, taper_v), (mask, mask_v), (fine, fine_v), (turns, turns_v)]
    small = [pltpu.make_async_copy(a, b, local.at[i]) for i, (a, b) in enumerate(small)]
    edge = 3 * tm
    quarters = [edge, 1, 2]
    fwd_copies = [pltpu.make_async_copy(forward.at[q], fwd.at[i], table_sem.at[i]) for i, q in enumerate(quarters)]
    inv_copies = [pltpu.make_async_copy(inverse.at[q], inv.at[i], table_sem.at[3 + i]) for i, q in enumerate(quarters)]
    for copy in small[:2] + fwd_copies + small[2:] + inv_copies:
        copy.start()

    outer = pl.multiple_of(2 * QUARTER * tm, QUARTER)
    shared = pl.multiple_of(2 * QUARTER * (1 - tm), QUARTER)

    def tapered(offset, quarter):
        weights = taper_v[:, pl.ds(pl.multiple_of(quarter * QUARTER, QUARTER), QUARTER)]
        return (sig[:, pl.ds(offset, QUARTER)].astype(F32) * weights).astype(BF16)

    shape = (2, 2, LAYERS, GROUP, LINES)
    small[0].wait()
    small[1].wait()
    both = jnp.concatenate([tapered(shared, edge), tapered(outer, edge)], axis=0)
    fwd_copies[0].wait()
    both = jnp.dot(both, fwd[0], preferred_element_type=F32)
    other_part[...] = both[:LINES].T.reshape(shape).astype(BF16)
    middle = [pl.multiple_of(QUARTER * (1 - tm), QUARTER), pl.multiple_of(QUARTER * (2 - tm), QUARTER)]
    total = both[LINES:]
    for i in range(2):
        fwd_copies[1 + i].wait()
        total += jnp.dot(tapered(middle[i], 1 + i), fwd[1 + i], preferred_element_type=F32)
    own_part[...] = total.T.reshape(shape)
    own_send[...] = own_part[1 - x].astype(BF16)

    pl.semaphore_wait(barrier, PLANE + 2)
    sums = []
    for pair in range(2):
        for k, layer in enumerate(layers):
            sources = (other_part.at[x, pair, layer], own_send.at[pair, layer], other_part.at[1 - x, pair, layer])
            sums.append(
                [
                    pltpu.make_async_remote_copy(
                        source, summands.at[i, pair, layer], sum_send, sum_recv.at[pair, i, k],
                        device_id=peer, device_id_type=MESH,
                    )
                    for i, (source, peer) in enumerate(zip(sources, (partner, far, diagonal)))
                ]
            )
            if pair * LAYERS + k < AHEAD:
                for i in (1, 2, 0):
                    sums[-1][i].start()

    def spread(source, target, pair, group, send, recv):
        for place, d in group:
            pltpu.make_async_remote_copy(
                source.at[pair, place], target.at[pair, here], send, recv,
                device_id={"chan": d}, device_id_type=MESH,
            ).start()

    def rows(tiles):
        return tiles.reshape(AROUND // 2, ROWS, LINES)

    for pair in range(2):
        for k, layer in enumerate(layers):
            step = pair * LAYERS + k
            for copy in sums[step]:
                copy.wait_recv()
            if step + AHEAD < 2 * LAYERS:
                for i in (1, 2, 0):
                    sums[step + AHEAD][i].start()
            mine = own_part[x, pair, layer] + summands[0, pair, layer].astype(F32)
            theirs = summands[1, pair, layer].astype(F32) + summands[2, pair, layer].astype(F32)
            low, high = jnp.where(x == 0, mine, theirs), jnp.where(x == 0, theirs, mine)
            even, odd = regroup(rows(low), rows(high))
            tiles = jnp.stack([even, odd], axis=1).reshape(AROUND, ROWS, LINES)
            send1[pair, pl.ds(layer * AROUND, AROUND)] = tiles.astype(BF16)
            spread(send1, got1, pair, everyone[k], send_sem.at[0], recv1.at[pair])
        got1[pair, here] = send1[pair, here]

    for copy in small[2:]:
        copy.wait()
    passes = mask_v[pl.ds(me, 1), :].astype(F32) * (1.0 / LINES)
    cosine, sine = fine_v[2], fine_v[3]
    left = jnp.concatenate([cosine * passes, sine * passes], axis=1)
    right = jnp.concatenate(
        [jnp.concatenate([cosine, sine], axis=1), jnp.concatenate([sine, -cosine], axis=1)], axis=0
    )
    fan = jnp.dot(left, right, precision=lax.Precision.HIGHEST, preferred_element_type=F32)
    fan = jnp.concatenate(
        [fan, jnp.concatenate([-fan[:, LINES:], fan[:, :LINES]], axis=1)], axis=0
    )
    fan_high = fan.astype(BF16)
    fan_low = (fan - fan_high.astype(F32)).astype(BF16)

    twist_cos, twist_sin = fine_v[0], fine_v[1]

    def across_channels(pair):
        lines = lines_v.at[pair]
        lines[...] = got1[pair].astype(F32).reshape(PLANE * ROWS, LINES)

        def spot(half, imag, b):
            return pl.ds(half * ROWS // 2 + imag * PAIR + b, PLANE, stride=ROWS)

        picked = [
            [
                jnp.concatenate([lines[spot(h, imag, b), :] for h in range(2)], axis=0).astype(BF16)
                for b in range(PAIR)
            ]
            for imag in range(2)
        ]
        stacked = jnp.concatenate([jnp.concatenate(p, axis=1) for p in picked], axis=0)
        wave = jnp.dot(turns_v[0], stacked, preferred_element_type=F32)
        wave += jnp.dot(turns_v[1], stacked, preferred_element_type=F32)
        turned = []
        for b in range(PAIR):
            re = wave[:LINES, b * LINES : (b + 1) * LINES]
            im = wave[LINES:, b * LINES : (b + 1) * LINES]
            turned.append(
                jnp.concatenate(
                    [re * twist_cos + im * twist_sin, im * twist_cos - re * twist_sin], axis=1
                )
            )
        turned = jnp.concatenate(turned, axis=0)
        high = turned.astype(BF16)
        low = (turned - high.astype(F32)).astype(BF16)
        masked = jnp.dot(high, fan_high, preferred_element_type=F32)
        masked += jnp.dot(low, fan_high, preferred_element_type=F32)
        masked += jnp.dot(high, fan_low, preferred_element_type=F32)
        real, imag = [], []
        for b in range(PAIR):
            re = masked[b * LINES : (b + 1) * LINES, :LINES]
            im = masked[b * LINES : (b + 1) * LINES, LINES:]
            real.append(re * twist_cos - im * twist_sin)
            imag.append(im * twist_cos + re * twist_sin)
        straight = jnp.concatenate(
            [jnp.concatenate(real, axis=1), jnp.concatenate(imag, axis=1)], axis=0
        )
        high = straight.astype(BF16)
        low = (straight - high.astype(F32)).astype(BF16)
        back = jnp.dot(turns_v[2], high, preferred_element_type=F32)
        back += jnp.dot(turns_v[2], low, preferred_element_type=F32)
        back += jnp.dot(turns_v[3], high, preferred_element_type=F32)
        for h in range(2):
            for i in range(2):
                top = i * LINES + h * PLANE
                for b in range(PAIR):
                    lines[spot(h, i, b), :] = back[top : top + PLANE, b * LINES : (b + 1) * LINES]
        send2[pair] = lines[...].reshape(PLANE, ROWS, LINES).astype(BF16)

    rest = pl.ds(0, PLANE - 1)

    def transfer(ref, send, recv):
        return pltpu.make_async_remote_copy(
            ref, ref, send, recv, device_id=partner, device_id_type=MESH
        )

    for pair in range(2):
        transfer(got1.at[pair, rest], send_sem.at[0], recv1.at[pair]).wait_recv()
        across_channels(pair)
        for group in everyone:
            spread(send2, got2, pair, group, send_sem.at[1], recv2.at[pair, z])
        got2[pair, here] = send2[pair, here]

    for pair in range(2):
        for k, layer in enumerate(layers):
            count = pl.ds(0, len(everyone[k]))
            transfer(got2.at[pair, count], send_sem.at[1], recv2.at[pair, layer]).wait_recv()
            tiles = got2[pair, pl.ds(layer * AROUND, AROUND)].astype(F32)
            tiles = tiles.reshape(AROUND // 2, 2, ROWS, LINES)
            low, high = regroup(tiles[:, 0], tiles[:, 1])
            mine, theirs = jnp.where(x == 0, low, high), jnp.where(x == 0, high, low)
            kept[pair, layer] = mine.reshape(GROUP, LINES).astype(BF16)
            leaving[pair, layer] = theirs.reshape(GROUP, LINES).astype(BF16)
            for kind, source, peer in ((1, leaving, far), (2, leaving, diagonal), (0, kept, partner)):
                pltpu.make_async_remote_copy(
                    source.at[pair, layer], passed.at[kind, pair, layer], pass_send,
                    pass_recv.at[kind, pair], device_id=peer, device_id_type=MESH,
                ).start()

    def turn(block, target, half, pair):
        lines = block.astype(F32).reshape(BAND // 2, LINES).T
        column = half * BAND + pair * (BAND // 2)
        target[:, pl.ds(pl.multiple_of(column, BAND // 2), BAND // 2)] = lines.astype(BF16)

    def arrived(kind, target, half, pair):
        transfer(passed.at[kind, pair], pass_send, pass_recv.at[kind, pair]).wait_recv()
        turn(passed[kind, pair], target, half, pair)

    def frame(values, i):
        return jnp.dot(values, inv[i], preferred_element_type=F32) * (1.0 / WINDOW)

    for copy in inv_copies:
        copy.wait()
    for pair in range(2):
        turn(kept[pair], back_v, x, pair)
        arrived(1, back_v, 1 - x, pair)
    out[:, pl.ds(outer, QUARTER)] = frame(back_v[...], 0).astype(BF16)
    centre = 1 + tm
    out[:, QUARTER : 2 * QUARTER] = frame(back_v[...], centre).astype(BF16)
    overlap = frame(back_v[...], 2 - tm)
    for pair in range(2):
        arrived(2, other_v, 1 - x, pair)
        arrived(0, other_v, x, pair)
    out[:, pl.ds(shared, QUARTER)] = (overlap + frame(other_v[...], 0)).astype(BF16)
    transfer(summands, sum_send, recv1.at[0]).wait_send()
    transfer(send1.at[:, rest], send_sem.at[0], recv1.at[0]).wait_send()
    transfer(send2.at[:, rest], send_sem.at[1], recv1.at[0]).wait_send()
    transfer(passed, pass_send, recv1.at[0]).wait_send()


def on_device(signal, fan_mask):
    far = pl.BlockSpec(memory_space=pltpu.HBM)
    block = (2, PLANE, ROWS, LINES)
    spectra = (2, LAYERS, GROUP, LINES)
    dma = pltpu.SemaphoreType.DMA
    vmem = pltpu.VMEM
    return pl.pallas_call(
        kernel,
        out_shape=jax.ShapeDtypeStruct(signal.shape, BF16),
        in_specs=[far] * 7,
        out_specs=pl.BlockSpec(memory_space=pltpu.VMEM),
        scratch_shapes=[
            vmem(signal.shape, BF16),
            vmem((LINES, LINES), jnp.int32),
            vmem((3, QUARTER, 2 * BAND), BF16),
            vmem((3, 2 * BAND, QUARTER), BF16),
            vmem((1, WINDOW), F32),
            vmem((4, 2 * LINES, 2 * LINES), BF16),
            vmem((4, LINES, LINES), F32),
            vmem((2, *spectra), F32),
            vmem(spectra, BF16),
            vmem((2, *spectra), BF16),
            vmem((3, *spectra), BF16),
            vmem(block, BF16),
            vmem(block, BF16),
            vmem(block, BF16),
            vmem(block, BF16),
            vmem(spectra, BF16),
            vmem(spectra, BF16),
            vmem((3, *spectra), BF16),
            vmem((2, PLANE * ROWS, LINES), F32),
            vmem((LINES, 2 * BAND), BF16),
            vmem((LINES, 2 * BAND), BF16),
            dma((5,)),
            dma((6,)),
            dma(()),
            dma((2, 3, LAYERS)),
            dma((2,)),
            dma((2,)),
            dma((2, LAYERS)),
            dma(()),
            dma((3, 2)),
        ],
        compiler_params=pltpu.CompilerParams(
            collective_id=0, has_side_effects=True, vmem_limit_bytes=56 * 2**20
        ),
        cost_estimate=pl.CostEstimate(
            flops=5 * 10**9, bytes_accessed=20 * 10**6, transcendentals=0
        ),
    )(signal, fan_mask, *tables())


def solution(mesh):
    return jax.shard_map(
        on_device,
        mesh=mesh,
        in_specs=(P("chan", "tm"), P()),
        out_specs=P("chan", "tm"),
        check_vma=False,
    )
```

```python
import functools
import math

import jax
import jax.numpy as jnp
import ml_dtypes
import numpy as np
from jax import lax
from jax.experimental import pallas as pl
from jax.experimental.pallas import tpu as pltpu
from jax.sharding import PartitionSpec as P

WINDOW = 4096
BAND = 512
QUARTER = WINDOW // 4
LINES = 128
BINS = 4
PAIR = BINS // 2
ROWS = 2 * BINS
MESH = pl.DeviceIdType.MESH
F32 = jnp.float32
BF16 = jnp.bfloat16


def high_low(table):
    high = table.astype(ml_dtypes.bfloat16)
    low = (table - high.astype(np.float64)).astype(ml_dtypes.bfloat16)
    return high, low


def three_parts(table):
    rest, parts = table.astype(np.float32), []
    for _ in range(3):
        parts.append(rest.astype(ml_dtypes.bfloat16))
        rest = rest - parts[-1].astype(np.float32)
    return parts


@functools.cache
def tables():
    positions = np.arange(WINDOW)
    bins = np.arange(BAND)
    angle = 2.0 * math.pi / WINDOW * (positions[:, None] * bins[None, :] % WINDOW)
    cosine, sine = np.cos(angle), np.sin(angle)
    grid = np.arange(LINES).reshape(2, 4, LAYERS, 2)
    owners = grid.transpose(0, 2, 1, 3).reshape(LINES)
    places = [(WINDOW, 2, 2, PLANE, 2, PAIR), (0, 2, 4, 3, 1, 5)]
    forward = np.stack([cosine, -sine], axis=1).reshape(WINDOW, 2, LINES, BINS)[:, :, owners]
    forward = forward.reshape(places[0]).transpose(places[1]).reshape(4, QUARTER, 2 * BAND)
    weight = np.where(bins == 0, 1.0, 2.0)
    inverse = np.stack([weight * cosine, -weight * sine], axis=1)
    inverse = inverse.reshape(WINDOW, 2, LINES, BINS)[:, :, owners]
    inverse = inverse.reshape(places[0]).transpose(places[1]).reshape(4, QUARTER, 2 * BAND)
    inverse = inverse.transpose(0, 2, 1)
    taper = (0.5 - 0.5 * np.cos(2.0 * math.pi / WINDOW * positions)).reshape(4, QUARTER)
    lines = np.arange(LINES)
    angle = 2.0 * math.pi / LINES * (lines[:, None] * lines[None, :] % LINES)
    cosine, sine = np.cos(angle), np.sin(angle)
    order = np.r_[owners, LINES + owners]
    analysis = np.block([[cosine, sine], [-sine, cosine]])[:, order]
    synthesis = np.block([[cosine, -sine], [sine, cosine]])[order] / LINES
    turns = np.stack(high_low(analysis) + high_low(synthesis))
    angle = 2.0 * math.pi / LINES**2 * (lines[:, None] * lines[None, :])
    fine = np.stack([np.cos(angle), np.sin(angle), cosine, sine])
    taper = np.concatenate([np.pad(part, ((0, 12), (0, 0))) for part in three_parts(taper)])
    blocks = [part[i] for i in range(4) for part in three_parts(fine)] + [np.zeros_like(cosine)] * 4
    fine = np.concatenate([np.concatenate(blocks[k : k + 8], axis=1) for k in (0, 8)])
    rows = [taper, fine, np.concatenate(list(turns), axis=1), *forward, *inverse]
    return np.concatenate([part.astype(ml_dtypes.bfloat16) for part in rows])


LAYERS = 8
AROUND = 8
PLANE = LAYERS * AROUND
TAPER_ROWS = 48
PACKED = TAPER_ROWS + 4 * LINES
GROUP = AROUND * 2 * PAIR
Z_STEPS = (4, 3, 5, 2, 6, 1, 7, 0)
AHEAD = 8
Y_STEPS = ((2, 1), (2, 0), (1, 1), (3, 1), (1, 0), (3, 0), (0, 1), (0, 0))


def regroup(first, second):
    upper = jnp.concatenate([first[:, :4], second[:, :4]], axis=1)
    return upper, jnp.concatenate([first[:, 4:], second[:, 4:]], axis=1)


def kernel(
    signal, mask, table, out,
    sig, mask_v, fwd, inv, packed, taper_v, fine_v, own_part, own_send, other_part, summands,
    send1, got1, send2, got2, kept, leaving, passed, lines_v, frames,
    local, table_sem, sum_send, sum_recv, send_sem, recv1, recv2, pass_send, pass_recv,
):
    me, tm = lax.axis_index("chan"), lax.axis_index("tm")
    rem, div = lax.rem, lax.div
    core, z, y, x = rem(me, 2), rem(div(me, 2), 8), rem(div(me, 16), 4), div(me, 64)
    layers = [rem(z + k, LAYERS) for k in Z_STEPS]
    spots = [(rem(y + j, 4), rem(core + c, 2)) for j, c in Y_STEPS]
    here = (z * 4 + y) * 2 + core
    across = me + PLANE * (1 - 2 * x)
    partner, far, diagonal = {"tm": 1 - tm}, {"chan": across}, {"chan": across, "tm": 1 - tm}

    everyone = []
    for k, layer in enumerate(layers):
        group = spots if Z_STEPS[k] else spots[:-1]
        everyone.append([((layer * 4 + j) * 2 + c, ((x * 4 + j) * 8 + layer) * 2 + c) for j, c in group])

    barrier = pltpu.get_barrier_semaphore()
    for peer in (far, diagonal, partner):
        pl.semaphore_signal(barrier, 1, device_id=peer, device_id_type=MESH)
    for group in everyone:
        for _, d in group:
            pl.semaphore_signal(barrier, 1, device_id={"chan": d}, device_id_type=MESH)

    edge = 3 * tm
    quarters = [edge, 1, 2]

    def part_of_table(start, size, target, sem):
        start = pl.multiple_of(start, 16)
        return pltpu.make_async_copy(table.at[pl.ds(start, size)], target, sem)

    small = [
        pltpu.make_async_copy(signal, sig, local.at[0]),
        part_of_table(0, TAPER_ROWS, packed.at[:TAPER_ROWS], local.at[1]),
        part_of_table(TAPER_ROWS, PACKED - TAPER_ROWS, packed.at[TAPER_ROWS:], local.at[2]),
        pltpu.make_async_copy(mask, mask_v, local.at[3]),
    ]
    fwd_copies = [
        part_of_table(PACKED + q * QUARTER, QUARTER, fwd.at[i], table_sem.at[i])
        for i, q in enumerate(quarters)
    ]
    inv_copies = [
        part_of_table(PACKED + (4 + q) * QUARTER, QUARTER, inv.at[i], table_sem.at[3 + i])
        for i, q in enumerate(quarters)
    ]
    for copy in small[:2] + fwd_copies + small[2:] + inv_copies:
        copy.start()

    outer = pl.multiple_of(2 * QUARTER * tm, QUARTER)
    shared = pl.multiple_of(2 * QUARTER * (1 - tm), QUARTER)

    def tapered(offset, quarter):
        weights = taper_v[pl.ds(quarter, 1), :]
        return (sig[:, pl.ds(offset, QUARTER)].astype(F32) * weights).astype(BF16)

    shape = (2, 2, LAYERS, GROUP, LINES)
    small[0].wait()
    small[1].wait()
    parts = [packed[16 * i : 16 * (i + 1), :].astype(F32) for i in range(3)]
    taper_v[...] = parts[0] + parts[1] + parts[2]
    both = jnp.concatenate([tapered(shared, edge), tapered(outer, edge)], axis=0)
    fwd_copies[0].wait()
    both = jnp.dot(both, fwd[0], preferred_element_type=F32)
    other_part[...] = both[:LINES].T.reshape(shape).astype(BF16)
    middle = [pl.multiple_of(QUARTER * (1 - tm), QUARTER), pl.multiple_of(QUARTER * (2 - tm), QUARTER)]
    total = both[LINES:]
    for i in range(2):
        fwd_copies[1 + i].wait()
        total += jnp.dot(tapered(middle[i], 1 + i), fwd[1 + i], preferred_element_type=F32)
    own_part[...] = total.T.reshape(shape)
    own_send[...] = own_part[1 - x].astype(BF16)

    pl.semaphore_wait(barrier, PLANE + 2)
    sums = []
    for pair in range(2):
        for k, layer in enumerate(layers):
            sources = (other_part.at[x, pair, layer], own_send.at[pair, layer], other_part.at[1 - x, pair, layer])
            sums.append(
                [
                    pltpu.make_async_remote_copy(
                        source, summands.at[i, pair, layer], sum_send, sum_recv.at[pair, i, k],
                        device_id=peer, device_id_type=MESH,
                    )
                    for i, (source, peer) in enumerate(zip(sources, (partner, far, diagonal)))
                ]
            )
            if pair * LAYERS + k < AHEAD:
                for i in (1, 2, 0):
                    sums[-1][i].start()

    def spread(source, target, pair, group, send, recv):
        for place, d in group:
            pltpu.make_async_remote_copy(
                source.at[pair, place], target.at[pair, here], send, recv,
                device_id={"chan": d}, device_id_type=MESH,
            ).start()

    def rows(tiles):
        return tiles.reshape(AROUND // 2, ROWS, LINES)

    for pair in range(2):
        for k, layer in enumerate(layers):
            step = pair * LAYERS + k
            for copy in sums[step]:
                copy.wait_recv()
            if step + AHEAD < 2 * LAYERS:
                for i in (1, 2, 0):
                    sums[step + AHEAD][i].start()
            mine = own_part[x, pair, layer] + summands[0, pair, layer].astype(F32)
            theirs = summands[1, pair, layer].astype(F32) + summands[2, pair, layer].astype(F32)
            low, high = jnp.where(x == 0, mine, theirs), jnp.where(x == 0, theirs, mine)
            even, odd = regroup(rows(low), rows(high))
            tiles = jnp.stack([even, odd], axis=1).reshape(AROUND, ROWS, LINES)
            send1[pair, pl.ds(layer * AROUND, AROUND)] = tiles.astype(BF16)
            spread(send1, got1, pair, everyone[k], send_sem.at[0], recv1.at[pair])
        got1[pair, here] = send1[pair, here]

    for copy in small[2:]:
        copy.wait()
    for i in range(4):
        parts = []
        for k in range(3 * i, 3 * i + 3):
            top, column = TAPER_ROWS + k // 8 * LINES, k % 8 * LINES
            parts.append(packed[top : top + LINES, column : column + LINES].astype(F32))
        fine_v[i] = parts[0] + parts[1] + parts[2]
    turns = [packed[PACKED - 2 * LINES :, 2 * LINES * i : 2 * LINES * (i + 1)] for i in range(4)]
    passes = mask_v[pl.ds(me, 1), :].astype(F32) * (1.0 / LINES)
    cosine, sine = fine_v[2], fine_v[3]
    left = jnp.concatenate([cosine * passes, sine * passes], axis=1)
    right = jnp.concatenate(
        [jnp.concatenate([cosine, sine], axis=1), jnp.concatenate([sine, -cosine], axis=1)], axis=0
    )
    fan = jnp.dot(left, right, precision=lax.Precision.HIGHEST, preferred_element_type=F32)
    fan = jnp.concatenate(
        [fan, jnp.concatenate([-fan[:, LINES:], fan[:, :LINES]], axis=1)], axis=0
    )
    fan_high = fan.astype(BF16)
    fan_low = (fan - fan_high.astype(F32)).astype(BF16)

    twist_cos, twist_sin = fine_v[0], fine_v[1]

    def across_channels(pair):
        lines = lines_v.at[pair]
        lines[...] = got1[pair].astype(F32).reshape(PLANE * ROWS, LINES)

        def spot(half, imag, b):
            return pl.ds(half * ROWS // 2 + imag * PAIR + b, PLANE, stride=ROWS)

        picked = [
            [
                jnp.concatenate([lines[spot(h, imag, b), :] for h in range(2)], axis=0).astype(BF16)
                for b in range(PAIR)
            ]
            for imag in range(2)
        ]
        stacked = jnp.concatenate([jnp.concatenate(p, axis=1) for p in picked], axis=0)
        wave = jnp.dot(turns[0], stacked, preferred_element_type=F32)
        wave += jnp.dot(turns[1], stacked, preferred_element_type=F32)
        turned = []
        for b in range(PAIR):
            re = wave[:LINES, b * LINES : (b + 1) * LINES]
            im = wave[LINES:, b * LINES : (b + 1) * LINES]
            turned.append(
                jnp.concatenate(
                    [re * twist_cos + im * twist_sin, im * twist_cos - re * twist_sin], axis=1
                )
            )
        turned = jnp.concatenate(turned, axis=0)
        high = turned.astype(BF16)
        low = (turned - high.astype(F32)).astype(BF16)
        masked = jnp.dot(high, fan_high, preferred_element_type=F32)
        masked += jnp.dot(low, fan_high, preferred_element_type=F32)
        masked += jnp.dot(high, fan_low, preferred_element_type=F32)
        real, imag = [], []
        for b in range(PAIR):
            re = masked[b * LINES : (b + 1) * LINES, :LINES]
            im = masked[b * LINES : (b + 1) * LINES, LINES:]
            real.append(re * twist_cos - im * twist_sin)
            imag.append(im * twist_cos + re * twist_sin)
        straight = jnp.concatenate(
            [jnp.concatenate(real, axis=1), jnp.concatenate(imag, axis=1)], axis=0
        )
        high = straight.astype(BF16)
        low = (straight - high.astype(F32)).astype(BF16)
        back = jnp.dot(turns[2], high, preferred_element_type=F32)
        back += jnp.dot(turns[2], low, preferred_element_type=F32)
        back += jnp.dot(turns[3], high, preferred_element_type=F32)
        for h in range(2):
            for i in range(2):
                top = i * LINES + h * PLANE
                for b in range(PAIR):
                    lines[spot(h, i, b), :] = back[top : top + PLANE, b * LINES : (b + 1) * LINES]
        send2[pair] = lines[...].reshape(PLANE, ROWS, LINES).astype(BF16)

    rest = pl.ds(0, PLANE - 1)

    def transfer(ref, send, recv):
        return pltpu.make_async_remote_copy(
            ref, ref, send, recv, device_id=partner, device_id_type=MESH
        )

    for pair in range(2):
        transfer(got1.at[pair, rest], send_sem.at[0], recv1.at[pair]).wait_recv()
        across_channels(pair)
        for group in reversed(everyone):
            spread(send2, got2, pair, group, send_sem.at[1], recv2.at[pair, z])
        got2[pair, here] = send2[pair, here]

    for pair in range(2):
        for k, layer in reversed(list(enumerate(layers))):
            count = pl.ds(0, len(everyone[k]))
            transfer(got2.at[pair, count], send_sem.at[1], recv2.at[pair, layer]).wait_recv()
            tiles = got2[pair, pl.ds(layer * AROUND, AROUND)].astype(F32)
            tiles = tiles.reshape(AROUND // 2, 2, ROWS, LINES)
            low, high = regroup(tiles[:, 0], tiles[:, 1])
            mine, theirs = jnp.where(x == 0, low, high), jnp.where(x == 0, high, low)
            kept[pair, layer] = mine.reshape(GROUP, LINES).astype(BF16)
            leaving[pair, layer] = theirs.reshape(GROUP, LINES).astype(BF16)
            for kind, source, peer in ((1, leaving, far), (2, leaving, diagonal), (0, kept, partner)):
                pltpu.make_async_remote_copy(
                    source.at[pair, layer], passed.at[kind, pair, layer], pass_send,
                    pass_recv.at[kind, pair], device_id=peer, device_id_type=MESH,
                ).start()

    places = ((0, 0), (1, 1 + tm), (2, 2 - tm))

    def terms(block, half, pair, quarters):
        lines = block.astype(F32).reshape(BAND // 2, LINES).T.astype(BF16)
        rows = pl.ds(pl.multiple_of((2 * half + pair) * (BAND // 2), BAND // 2), BAND // 2)
        return [jnp.dot(lines, inv[i, rows, :], preferred_element_type=F32) for i in quarters]

    def arrived(kind, pair):
        transfer(passed.at[kind, pair], pass_send, pass_recv.at[kind, pair]).wait_recv()
        return passed[kind, pair]

    def put(column, value):
        out[:, pl.ds(column, QUARTER)] = (value * (1.0 / WINDOW)).astype(BF16)

    for copy in inv_copies:
        copy.wait()
    mine = [i for _, i in places]
    for k, term in enumerate(terms(kept[0], x, 0, mine)):
        frames[k] = term
    for k, term in enumerate(terms(kept[1], x, 1, mine)):
        frames[k] += term
    for k, term in enumerate(terms(arrived(1, 0), 1 - x, 0, mine)):
        frames[k] += term
    frames[2] += terms(arrived(2, 0), 1 - x, 0, [0])[0] + terms(arrived(0, 0), x, 0, [0])[0]
    last = terms(arrived(1, 1), 1 - x, 1, mine)
    put(outer, frames[0] + last[0])
    put(QUARTER, frames[1] + last[1])
    frames[2] += last[2]
    last = terms(arrived(2, 1), 1 - x, 1, [0])[0] + terms(arrived(0, 1), x, 1, [0])[0]
    put(shared, frames[2] + last)
    transfer(summands, sum_send, recv1.at[0]).wait_send()
    transfer(send1.at[:, rest], send_sem.at[0], recv1.at[0]).wait_send()
    transfer(send2.at[:, rest], send_sem.at[1], recv1.at[0]).wait_send()
    transfer(passed, pass_send, recv1.at[0]).wait_send()


def on_device(signal, fan_mask):
    far = pl.BlockSpec(memory_space=pltpu.HBM)
    block = (2, PLANE, ROWS, LINES)
    spectra = (2, LAYERS, GROUP, LINES)
    dma = pltpu.SemaphoreType.DMA
    vmem = pltpu.VMEM
    return pl.pallas_call(
        kernel,
        out_shape=jax.ShapeDtypeStruct(signal.shape, BF16),
        in_specs=[far] * 3,
        out_specs=pl.BlockSpec(memory_space=pltpu.VMEM),
        scratch_shapes=[
            vmem(signal.shape, BF16),
            vmem((LINES, LINES), jnp.int32),
            vmem((3, QUARTER, 2 * BAND), BF16),
            vmem((3, 2 * BAND, QUARTER), BF16),
            vmem((PACKED, 2 * BAND), BF16),
            vmem((16, QUARTER), F32),
            vmem((4, LINES, LINES), F32),
            vmem((2, *spectra), F32),
            vmem(spectra, BF16),
            vmem((2, *spectra), BF16),
            vmem((3, *spectra), BF16),
            vmem(block, BF16),
            vmem(block, BF16),
            vmem(block, BF16),
            vmem(block, BF16),
            vmem(spectra, BF16),
            vmem(spectra, BF16),
            vmem((3, *spectra), BF16),
            vmem((2, PLANE * ROWS, LINES), F32),
            vmem((3, LINES, QUARTER), F32),
            dma((4,)),
            dma((6,)),
            dma(()),
            dma((2, 3, LAYERS)),
            dma((2,)),
            dma((2,)),
            dma((2, LAYERS)),
            dma(()),
            dma((3, 2)),
        ],
        compiler_params=pltpu.CompilerParams(
            collective_id=0, has_side_effects=True, vmem_limit_bytes=53 * 2**20
        ),
        cost_estimate=pl.CostEstimate(
            flops=5 * 10**9, bytes_accessed=20 * 10**6, transcendentals=0
        ),
    )(signal, fan_mask, tables())


def solution(mesh):
    return jax.shard_map(
        on_device,
        mesh=mesh,
        in_specs=(P("chan", "tm"), P()),
        out_specs=P("chan", "tm"),
        check_vma=False,
    )
```

```python
import functools
import math

import jax
import jax.numpy as jnp
import ml_dtypes
import numpy as np
from jax import lax
from jax.experimental import pallas as pl
from jax.experimental.pallas import tpu as pltpu
from jax.sharding import PartitionSpec as P

WINDOW = 4096
BAND = 512
QUARTER = WINDOW // 4
LINES = 128
BINS = 4
PAIR = BINS // 2
ROWS = 2 * BINS
MESH = pl.DeviceIdType.MESH
F32 = jnp.float32
BF16 = jnp.bfloat16


def high_low(table):
    high = table.astype(ml_dtypes.bfloat16)
    low = (table - high.astype(np.float64)).astype(ml_dtypes.bfloat16)
    return high, low


def three_parts(table):
    rest, parts = table.astype(np.float32), []
    for _ in range(3):
        parts.append(rest.astype(ml_dtypes.bfloat16))
        rest = rest - parts[-1].astype(np.float32)
    return parts


@functools.cache
def tables():
    positions = np.arange(WINDOW)
    bins = np.arange(BAND)
    angle = 2.0 * math.pi / WINDOW * (positions[:, None] * bins[None, :] % WINDOW)
    cosine, sine = np.cos(angle), np.sin(angle)
    grid = np.arange(LINES).reshape(2, 4, LAYERS, 2)
    owners = grid.transpose(0, 2, 1, 3).reshape(LINES)
    places = [(WINDOW, 2, 2, PLANE, 2, PAIR), (0, 2, 4, 3, 1, 5)]
    forward = np.stack([cosine, -sine], axis=1).reshape(WINDOW, 2, LINES, BINS)[:, :, owners]
    forward = forward.reshape(places[0]).transpose(places[1]).reshape(4, QUARTER, 2 * BAND)
    weight = np.where(bins == 0, 1.0, 2.0)
    inverse = np.stack([weight * cosine, -weight * sine], axis=1)
    inverse = inverse.reshape(WINDOW, 2, LINES, BINS)[:, :, owners]
    inverse = inverse.reshape(places[0]).transpose(places[1]).reshape(4, QUARTER, 2 * BAND)
    inverse = inverse.transpose(0, 2, 1)
    taper = (0.5 - 0.5 * np.cos(2.0 * math.pi / WINDOW * positions)).reshape(4, QUARTER)
    lines = np.arange(LINES)
    angle = 2.0 * math.pi / LINES * (lines[:, None] * lines[None, :] % LINES)
    cosine, sine = np.cos(angle), np.sin(angle)
    order = np.r_[owners, LINES + owners]
    analysis = np.block([[cosine, sine], [-sine, cosine]])[:, order]
    synthesis = np.block([[cosine, -sine], [sine, cosine]])[order] / LINES
    turns = np.stack(high_low(analysis) + high_low(synthesis))
    angle = 2.0 * math.pi / LINES**2 * (lines[:, None] * lines[None, :])
    fine = np.stack([np.cos(angle), np.sin(angle), cosine, sine])
    taper = np.concatenate([np.pad(part, ((0, 12), (0, 0))) for part in three_parts(taper)])
    blocks = [part[i] for i in range(4) for part in three_parts(fine)] + [np.zeros_like(cosine)] * 4
    fine = np.concatenate([np.concatenate(blocks[k : k + 8], axis=1) for k in (0, 8)])
    rows = [taper, fine, np.concatenate(list(turns), axis=1), *forward, *inverse]
    return np.concatenate([part.astype(ml_dtypes.bfloat16) for part in rows])


LAYERS = 8
AROUND = 8
PLANE = LAYERS * AROUND
TAPER_ROWS = 48
PACKED = TAPER_ROWS + 4 * LINES
GROUP = AROUND * 2 * PAIR
Z_STEPS = (4, 3, 5, 2, 6, 1, 7, 0)
AHEAD = 8
Y_STEPS = ((2, 1), (2, 0), (1, 1), (3, 1), (1, 0), (3, 0), (0, 1), (0, 0))


def regroup(first, second):
    upper = jnp.concatenate([first[:, :4], second[:, :4]], axis=1)
    return upper, jnp.concatenate([first[:, 4:], second[:, 4:]], axis=1)


def kernel(
    signal, mask, table, out,
    sig, mask_v, fwd, inv, packed, taper_v, fine_v, fan_v, own_part, own_send, other_part, summands,
    send1, got1, send2, got2, kept, leaving, passed, lines_v, frames,
    local, table_sem, sum_send, sum_recv, send_sem, recv1, recv2, pass_send, pass_recv,
):
    me, tm = lax.axis_index("chan"), lax.axis_index("tm")
    rem, div = lax.rem, lax.div
    core, z, y, x = rem(me, 2), rem(div(me, 2), 8), rem(div(me, 16), 4), div(me, 64)
    layers = [rem(z + k, LAYERS) for k in Z_STEPS]
    spots = [(rem(y + j, 4), rem(core + c, 2)) for j, c in Y_STEPS]
    here = (z * 4 + y) * 2 + core
    across = me + PLANE * (1 - 2 * x)
    partner, far, diagonal = {"tm": 1 - tm}, {"chan": across}, {"chan": across, "tm": 1 - tm}

    everyone = []
    for k, layer in enumerate(layers):
        group = spots if Z_STEPS[k] else spots[:-1]
        everyone.append([((layer * 4 + j) * 2 + c, ((x * 4 + j) * 8 + layer) * 2 + c) for j, c in group])

    barrier = pltpu.get_barrier_semaphore()
    for peer in (far, diagonal, partner):
        pl.semaphore_signal(barrier, 1, device_id=peer, device_id_type=MESH)
    for group in everyone:
        for _, d in group:
            pl.semaphore_signal(barrier, 1, device_id={"chan": d}, device_id_type=MESH)

    edge = 3 * tm
    quarters = [edge, 1, 2]

    def part_of_table(start, size, target, sem):
        start = pl.multiple_of(start, 16)
        return pltpu.make_async_copy(table.at[pl.ds(start, size)], target, sem)

    small = [
        pltpu.make_async_copy(signal, sig, local.at[0]),
        part_of_table(0, TAPER_ROWS, packed.at[:TAPER_ROWS], local.at[1]),
        part_of_table(TAPER_ROWS, PACKED - TAPER_ROWS, packed.at[TAPER_ROWS:], local.at[2]),
        pltpu.make_async_copy(mask, mask_v, local.at[3]),
    ]
    fwd_copies = [
        part_of_table(PACKED + q * QUARTER, QUARTER, fwd.at[i], table_sem.at[i])
        for i, q in enumerate(quarters)
    ]
    inv_copies = [
        part_of_table(PACKED + (4 + q) * QUARTER, QUARTER, inv.at[i], table_sem.at[3 + i])
        for i, q in enumerate(quarters)
    ]
    for copy in small[:2] + fwd_copies + small[2:] + inv_copies:
        copy.start()

    outer = pl.multiple_of(2 * QUARTER * tm, QUARTER)
    shared = pl.multiple_of(2 * QUARTER * (1 - tm), QUARTER)

    def tapered(offset, quarter):
        weights = taper_v[pl.ds(quarter, 1), :]
        return (sig[:, pl.ds(offset, QUARTER)].astype(F32) * weights).astype(BF16)

    shape = (2, 2, LAYERS, GROUP, LINES)
    small[0].wait()
    small[1].wait()
    parts = [packed[16 * i : 16 * (i + 1), :].astype(F32) for i in range(3)]
    taper_v[...] = parts[0] + parts[1] + parts[2]
    both = jnp.concatenate([tapered(shared, edge), tapered(outer, edge)], axis=0)
    fwd_copies[0].wait()
    both = jnp.dot(both, fwd[0], preferred_element_type=F32)
    other_part[...] = both[:LINES].T.reshape(shape).astype(BF16)
    middle = [pl.multiple_of(QUARTER * (1 - tm), QUARTER), pl.multiple_of(QUARTER * (2 - tm), QUARTER)]
    total = both[LINES:]
    for i in range(2):
        fwd_copies[1 + i].wait()
        total += jnp.dot(tapered(middle[i], 1 + i), fwd[1 + i], preferred_element_type=F32)
    own_part[...] = total.T.reshape(shape)
    own_send[...] = own_part[1 - x].astype(BF16)

    pl.semaphore_wait(barrier, PLANE + 2)
    sums = []
    for pair in range(2):
        for k, layer in enumerate(layers):
            sources = (other_part.at[x, pair, layer], own_send.at[pair, layer], other_part.at[1 - x, pair, layer])
            sums.append(
                [
                    pltpu.make_async_remote_copy(
                        source, summands.at[i, pair, layer], sum_send, sum_recv.at[pair, i, k],
                        device_id=peer, device_id_type=MESH,
                    )
                    for i, (source, peer) in enumerate(zip(sources, (partner, far, diagonal)))
                ]
            )
            if pair * LAYERS + k < AHEAD:
                for i in (1, 2, 0):
                    sums[-1][i].start()

    def spread(source, target, pair, group, send, recv):
        for place, d in group:
            pltpu.make_async_remote_copy(
                source.at[pair, place], target.at[pair, here], send, recv,
                device_id={"chan": d}, device_id_type=MESH,
            ).start()

    def rows(tiles):
        return tiles.reshape(AROUND // 2, ROWS, LINES)

    for copy in small[2:]:
        copy.wait()
    for i in range(4):
        parts = []
        for k in range(3 * i, 3 * i + 3):
            top, column = TAPER_ROWS + k // 8 * LINES, k % 8 * LINES
            parts.append(packed[top : top + LINES, column : column + LINES].astype(F32))
        fine_v[i] = parts[0] + parts[1] + parts[2]
    passes = mask_v[pl.ds(me, 1), :].astype(F32) * (1.0 / LINES)
    cosine, sine = fine_v[2], fine_v[3]
    left = jnp.concatenate([cosine * passes, sine * passes], axis=1)
    right = jnp.concatenate(
        [jnp.concatenate([cosine, sine], axis=1), jnp.concatenate([sine, -cosine], axis=1)], axis=0
    )
    fan = jnp.dot(left, right, precision=lax.Precision.HIGHEST, preferred_element_type=F32)
    fan = jnp.concatenate(
        [fan, jnp.concatenate([-fan[:, LINES:], fan[:, :LINES]], axis=1)], axis=0
    )
    fan_v[0] = fan.astype(BF16)
    fan_v[1] = (fan - fan.astype(BF16).astype(F32)).astype(BF16)

    for pair in range(2):
        for k, layer in enumerate(layers):
            step = pair * LAYERS + k
            for copy in sums[step]:
                copy.wait_recv()
            if step + AHEAD < 2 * LAYERS:
                for i in (1, 2, 0):
                    sums[step + AHEAD][i].start()
            mine = own_part[x, pair, layer] + summands[0, pair, layer].astype(F32)
            theirs = summands[1, pair, layer].astype(F32) + summands[2, pair, layer].astype(F32)
            low, high = jnp.where(x == 0, mine, theirs), jnp.where(x == 0, theirs, mine)
            even, odd = regroup(rows(low), rows(high))
            tiles = jnp.stack([even, odd], axis=1).reshape(AROUND, ROWS, LINES)
            send1[pair, pl.ds(layer * AROUND, AROUND)] = tiles.astype(BF16)
            spread(send1, got1, pair, everyone[k], send_sem.at[0], recv1.at[pair])
        got1[pair, here] = send1[pair, here]

    turns = [packed[PACKED - 2 * LINES :, 2 * LINES * i : 2 * LINES * (i + 1)] for i in range(4)]
    twist_cos, twist_sin = fine_v[0], fine_v[1]

    def across_channels(pair):
        lines = lines_v.at[pair]
        lines[...] = got1[pair].astype(F32).reshape(PLANE * ROWS, LINES)

        def spot(half, imag, b):
            return pl.ds(half * ROWS // 2 + imag * PAIR + b, PLANE, stride=ROWS)

        picked = [
            [
                jnp.concatenate([lines[spot(h, imag, b), :] for h in range(2)], axis=0).astype(BF16)
                for b in range(PAIR)
            ]
            for imag in range(2)
        ]
        stacked = jnp.concatenate([jnp.concatenate(p, axis=1) for p in picked], axis=0)
        wave = jnp.dot(turns[0], stacked, preferred_element_type=F32)
        wave += jnp.dot(turns[1], stacked, preferred_element_type=F32)
        turned = []
        for b in range(PAIR):
            re = wave[:LINES, b * LINES : (b + 1) * LINES]
            im = wave[LINES:, b * LINES : (b + 1) * LINES]
            turned.append(
                jnp.concatenate(
                    [re * twist_cos + im * twist_sin, im * twist_cos - re * twist_sin], axis=1
                )
            )
        turned = jnp.concatenate(turned, axis=0)
        high = turned.astype(BF16)
        low = (turned - high.astype(F32)).astype(BF16)
        masked = jnp.dot(high, fan_v[0], preferred_element_type=F32)
        masked += jnp.dot(low, fan_v[0], preferred_element_type=F32)
        masked += jnp.dot(high, fan_v[1], preferred_element_type=F32)
        real, imag = [], []
        for b in range(PAIR):
            re = masked[b * LINES : (b + 1) * LINES, :LINES]
            im = masked[b * LINES : (b + 1) * LINES, LINES:]
            real.append(re * twist_cos - im * twist_sin)
            imag.append(im * twist_cos + re * twist_sin)
        straight = jnp.concatenate(
            [jnp.concatenate(real, axis=1), jnp.concatenate(imag, axis=1)], axis=0
        )
        high = straight.astype(BF16)
        low = (straight - high.astype(F32)).astype(BF16)
        back = jnp.dot(turns[2], high, preferred_element_type=F32)
        back += jnp.dot(turns[2], low, preferred_element_type=F32)
        back += jnp.dot(turns[3], high, preferred_element_type=F32)
        for h in range(2):
            for i in range(2):
                top = i * LINES + h * PLANE
                for b in range(PAIR):
                    lines[spot(h, i, b), :] = back[top : top + PLANE, b * LINES : (b + 1) * LINES]
        send2[pair] = lines[...].reshape(PLANE, ROWS, LINES).astype(BF16)

    rest = pl.ds(0, PLANE - 1)

    def transfer(ref, send, recv):
        return pltpu.make_async_remote_copy(
            ref, ref, send, recv, device_id=partner, device_id_type=MESH
        )

    for pair in range(2):
        transfer(got1.at[pair, rest], send_sem.at[0], recv1.at[pair]).wait_recv()
        across_channels(pair)
        for group in reversed(everyone):
            spread(send2, got2, pair, group, send_sem.at[1], recv2.at[pair, z])
        got2[pair, here] = send2[pair, here]

    for pair in range(2):
        for k, layer in reversed(list(enumerate(layers))):
            count = pl.ds(0, len(everyone[k]))
            transfer(got2.at[pair, count], send_sem.at[1], recv2.at[pair, layer]).wait_recv()
            tiles = got2[pair, pl.ds(layer * AROUND, AROUND)].astype(F32)
            tiles = tiles.reshape(AROUND // 2, 2, ROWS, LINES)
            low, high = regroup(tiles[:, 0], tiles[:, 1])
            mine, theirs = jnp.where(x == 0, low, high), jnp.where(x == 0, high, low)
            kept[pair, layer] = mine.reshape(GROUP, LINES).astype(BF16)
            leaving[pair, layer] = theirs.reshape(GROUP, LINES).astype(BF16)
            for kind, source, peer in ((1, leaving, far), (2, leaving, diagonal), (0, kept, partner)):
                pltpu.make_async_remote_copy(
                    source.at[pair, layer], passed.at[kind, pair, layer], pass_send,
                    pass_recv.at[kind, pair], device_id=peer, device_id_type=MESH,
                ).start()

    places = ((0, 0), (1, 1 + tm), (2, 2 - tm))

    def terms(block, half, pair, quarters):
        lines = block.astype(F32).reshape(BAND // 2, LINES).T.astype(BF16)
        rows = pl.ds(pl.multiple_of((2 * half + pair) * (BAND // 2), BAND // 2), BAND // 2)
        return [jnp.dot(lines, inv[i, rows, :], preferred_element_type=F32) for i in quarters]

    def arrived(kind, pair):
        transfer(passed.at[kind, pair], pass_send, pass_recv.at[kind, pair]).wait_recv()
        return passed[kind, pair]

    def put(column, value):
        out[:, pl.ds(column, QUARTER)] = (value * (1.0 / WINDOW)).astype(BF16)

    for copy in inv_copies:
        copy.wait()
    mine = [i for _, i in places]
    for k, term in enumerate(terms(kept[0], x, 0, mine)):
        frames[k] = term
    for k, term in enumerate(terms(kept[1], x, 1, mine)):
        frames[k] += term
    for k, term in enumerate(terms(arrived(1, 0), 1 - x, 0, mine)):
        frames[k] += term
    frames[2] += terms(arrived(2, 0), 1 - x, 0, [0])[0] + terms(arrived(0, 0), x, 0, [0])[0]
    last = terms(arrived(1, 1), 1 - x, 1, mine)
    put(outer, frames[0] + last[0])
    put(QUARTER, frames[1] + last[1])
    frames[2] += last[2]
    last = terms(arrived(2, 1), 1 - x, 1, [0])[0] + terms(arrived(0, 1), x, 1, [0])[0]
    put(shared, frames[2] + last)
    transfer(summands, sum_send, recv1.at[0]).wait_send()
    transfer(send1.at[:, rest], send_sem.at[0], recv1.at[0]).wait_send()
    transfer(send2.at[:, rest], send_sem.at[1], recv1.at[0]).wait_send()
    transfer(passed, pass_send, recv1.at[0]).wait_send()


def on_device(signal, fan_mask):
    far = pl.BlockSpec(memory_space=pltpu.HBM)
    block = (2, PLANE, ROWS, LINES)
    spectra = (2, LAYERS, GROUP, LINES)
    dma = pltpu.SemaphoreType.DMA
    vmem = pltpu.VMEM
    return pl.pallas_call(
        kernel,
        out_shape=jax.ShapeDtypeStruct(signal.shape, BF16),
        in_specs=[far] * 3,
        out_specs=pl.BlockSpec(memory_space=pltpu.VMEM),
        scratch_shapes=[
            vmem(signal.shape, BF16),
            vmem((LINES, LINES), jnp.int32),
            vmem((3, QUARTER, 2 * BAND), BF16),
            vmem((3, 2 * BAND, QUARTER), BF16),
            vmem((PACKED, 2 * BAND), BF16),
            vmem((16, QUARTER), F32),
            vmem((4, LINES, LINES), F32),
            vmem((2, 2 * LINES, 2 * LINES), BF16),
            vmem((2, *spectra), F32),
            vmem(spectra, BF16),
            vmem((2, *spectra), BF16),
            vmem((3, *spectra), BF16),
            vmem(block, BF16),
            vmem(block, BF16),
            vmem(block, BF16),
            vmem(block, BF16),
            vmem(spectra, BF16),
            vmem(spectra, BF16),
            vmem((3, *spectra), BF16),
            vmem((2, PLANE * ROWS, LINES), F32),
            vmem((3, LINES, QUARTER), F32),
            dma((4,)),
            dma((6,)),
            dma(()),
            dma((2, 3, LAYERS)),
            dma((2,)),
            dma((2,)),
            dma((2, LAYERS)),
            dma(()),
            dma((3, 2)),
        ],
        compiler_params=pltpu.CompilerParams(
            collective_id=0, has_side_effects=True, vmem_limit_bytes=53 * 2**20
        ),
        cost_estimate=pl.CostEstimate(
            flops=5 * 10**9, bytes_accessed=20 * 10**6, transcendentals=0
        ),
    )(signal, fan_mask, tables())


def solution(mesh):
    return jax.shard_map(
        on_device,
        mesh=mesh,
        in_specs=(P("chan", "tm"), P()),
        out_specs=P("chan", "tm"),
        check_vma=False,
    )
```

```python
import functools
import math

import jax
import jax.numpy as jnp
import ml_dtypes
import numpy as np
from jax import lax
from jax.experimental import pallas as pl
from jax.experimental.pallas import tpu as pltpu
from jax.sharding import PartitionSpec as P

WINDOW = 4096
BAND = 512
QUARTER = WINDOW // 4
LINES = 128
BINS = 4
PAIR = BINS // 2
ROWS = 2 * BINS
MESH = pl.DeviceIdType.MESH
F32 = jnp.float32
BF16 = jnp.bfloat16


def high_low(table):
    high = table.astype(ml_dtypes.bfloat16)
    low = (table - high.astype(np.float64)).astype(ml_dtypes.bfloat16)
    return high, low


def three_parts(table):
    rest, parts = table.astype(np.float32), []
    for _ in range(3):
        parts.append(rest.astype(ml_dtypes.bfloat16))
        rest = rest - parts[-1].astype(np.float32)
    return parts


@functools.cache
def tables():
    positions = np.arange(WINDOW)
    bins = np.arange(BAND)
    angle = 2.0 * math.pi / WINDOW * (positions[:, None] * bins[None, :] % WINDOW)
    cosine, sine = np.cos(angle), np.sin(angle)
    grid = np.arange(LINES).reshape(2, 4, LAYERS, 2)
    owners = grid.transpose(0, 2, 1, 3).reshape(LINES)
    places = [(WINDOW, 2, 2, PLANE, 2, PAIR), (0, 2, 4, 3, 1, 5)]
    forward = np.stack([cosine, -sine], axis=1).reshape(WINDOW, 2, LINES, BINS)[:, :, owners]
    forward = forward.reshape(places[0]).transpose(places[1]).reshape(4, QUARTER, 2 * BAND)
    weight = np.where(bins == 0, 1.0, 2.0)
    inverse = np.stack([weight * cosine, -weight * sine], axis=1)
    inverse = inverse.reshape(WINDOW, 2, LINES, BINS)[:, :, owners]
    inverse = inverse.reshape(places[0]).transpose(places[1]).reshape(4, QUARTER, 2 * BAND)
    inverse = inverse.transpose(0, 2, 1)
    taper = (0.5 - 0.5 * np.cos(2.0 * math.pi / WINDOW * positions)).reshape(4, QUARTER)
    lines = np.arange(LINES)
    angle = 2.0 * math.pi / LINES * (lines[:, None] * lines[None, :] % LINES)
    cosine, sine = np.cos(angle), np.sin(angle)
    order = np.r_[owners, LINES + owners]
    analysis = np.block([[cosine, sine], [-sine, cosine]])[:, order]
    synthesis = np.block([[cosine, -sine], [sine, cosine]])[order] / LINES
    turns = np.stack(high_low(analysis) + high_low(synthesis))
    angle = 2.0 * math.pi / LINES**2 * (lines[:, None] * lines[None, :])
    fine = np.stack([np.cos(angle), np.sin(angle), cosine, sine])
    taper = np.concatenate([np.pad(part, ((0, 12), (0, 0))) for part in three_parts(taper)])
    blocks = [part[i] for i in range(4) for part in three_parts(fine)] + [np.zeros_like(cosine)] * 4
    fine = np.concatenate([np.concatenate(blocks[k : k + 8], axis=1) for k in (0, 8)])
    rows = [taper, fine, np.concatenate(list(turns), axis=1), *forward, *inverse]
    return np.concatenate([part.astype(ml_dtypes.bfloat16) for part in rows])


LAYERS = 8
AROUND = 8
PLANE = LAYERS * AROUND
TAPER_ROWS = 48
PACKED = TAPER_ROWS + 4 * LINES
GROUP = AROUND * 2 * PAIR
Z_STEPS = (4, 3, 5, 2, 6, 1, 7, 0)
AHEAD = 8
Y_STEPS = ((2, 1), (2, 0), (1, 1), (3, 1), (1, 0), (3, 0), (0, 1), (0, 0))


def regroup(first, second):
    upper = jnp.concatenate([first[:, :4], second[:, :4]], axis=1)
    return upper, jnp.concatenate([first[:, 4:], second[:, 4:]], axis=1)


def kernel(
    signal, mask, table, out,
    sig, mask_v, fwd, inv, packed, taper_v, fine_v, own_part, own_send, other_part, summands,
    send1, got1, send2, got2, split, passed, lines_v, frames,
    local, table_sem, sum_send, sum_recv, send_sem, recv1, recv2, pass_send, pass_recv,
):
    me, tm = lax.axis_index("chan"), lax.axis_index("tm")
    rem, div = lax.rem, lax.div
    core, z, y, x = rem(me, 2), rem(div(me, 2), 8), rem(div(me, 16), 4), div(me, 64)
    layers = [rem(z + k, LAYERS) for k in Z_STEPS]
    spots = [(rem(y + j, 4), rem(core + c, 2)) for j, c in Y_STEPS]
    here = (z * 4 + y) * 2 + core
    across = me + PLANE * (1 - 2 * x)
    partner, far, diagonal = {"tm": 1 - tm}, {"chan": across}, {"chan": across, "tm": 1 - tm}

    everyone = []
    for k, layer in enumerate(layers):
        group = spots if Z_STEPS[k] else spots[:-1]
        everyone.append([((layer * 4 + j) * 2 + c, ((x * 4 + j) * 8 + layer) * 2 + c) for j, c in group])

    barrier = pltpu.get_barrier_semaphore()
    for peer in (far, diagonal, partner):
        pl.semaphore_signal(barrier, 1, device_id=peer, device_id_type=MESH)
    for group in everyone:
        for _, d in group:
            pl.semaphore_signal(barrier, 1, device_id={"chan": d}, device_id_type=MESH)

    edge = 3 * tm
    quarters = [edge, 1, 2]

    def part_of_table(start, size, target, sem):
        start = pl.multiple_of(start, 16)
        return pltpu.make_async_copy(table.at[pl.ds(start, size)], target, sem)

    small = [
        pltpu.make_async_copy(signal, sig, local.at[0]),
        part_of_table(0, TAPER_ROWS, packed.at[:TAPER_ROWS], local.at[1]),
        part_of_table(TAPER_ROWS, PACKED - TAPER_ROWS, packed.at[TAPER_ROWS:], local.at[2]),
        pltpu.make_async_copy(mask, mask_v, local.at[3]),
    ]
    fwd_copies = [
        part_of_table(PACKED + q * QUARTER, QUARTER, fwd.at[i], table_sem.at[i])
        for i, q in enumerate(quarters)
    ]
    inv_copies = [
        part_of_table(PACKED + (4 + q) * QUARTER, QUARTER, inv.at[i], table_sem.at[3 + i])
        for i, q in enumerate(quarters)
    ]
    for copy in small[:2] + fwd_copies + small[2:] + inv_copies:
        copy.start()

    outer = pl.multiple_of(2 * QUARTER * tm, QUARTER)
    shared = pl.multiple_of(2 * QUARTER * (1 - tm), QUARTER)

    def tapered(offset, quarter):
        weights = taper_v[pl.ds(quarter, 1), :]
        return (sig[:, pl.ds(offset, QUARTER)].astype(F32) * weights).astype(BF16)

    shape = (2, 2, LAYERS, GROUP, LINES)
    small[0].wait()
    small[1].wait()
    parts = [packed[16 * i : 16 * (i + 1), :].astype(F32) for i in range(3)]
    taper_v[...] = parts[0] + parts[1] + parts[2]
    both = jnp.concatenate([tapered(shared, edge), tapered(outer, edge)], axis=0)
    fwd_copies[0].wait()
    both = jnp.dot(both, fwd[0], preferred_element_type=F32)
    other_part[...] = both[:LINES].T.reshape(shape).astype(BF16)
    middle = [pl.multiple_of(QUARTER * (1 - tm), QUARTER), pl.multiple_of(QUARTER * (2 - tm), QUARTER)]
    total = both[LINES:]
    for i in range(2):
        fwd_copies[1 + i].wait()
        total += jnp.dot(tapered(middle[i], 1 + i), fwd[1 + i], preferred_element_type=F32)
    own_part[...] = total.T.reshape(shape)
    own_send[...] = own_part[1 - x].astype(BF16)

    pl.semaphore_wait(barrier, PLANE + 2)
    sums = []
    for pair in range(2):
        for k, layer in enumerate(layers):
            sources = (other_part.at[x, pair, layer], own_send.at[pair, layer], other_part.at[1 - x, pair, layer])
            sums.append(
                [
                    pltpu.make_async_remote_copy(
                        source, summands.at[i, pair, layer], sum_send, sum_recv.at[pair, i, k],
                        device_id=peer, device_id_type=MESH,
                    )
                    for i, (source, peer) in enumerate(zip(sources, (partner, far, diagonal)))
                ]
            )
            if pair * LAYERS + k < AHEAD:
                for i in (1, 2, 0):
                    sums[-1][i].start()

    def spread(source, target, pair, group, send, recv):
        for place, d in group:
            pltpu.make_async_remote_copy(
                source.at[pair, place], target.at[pair, here], send, recv,
                device_id={"chan": d}, device_id_type=MESH,
            ).start()

    def rows(tiles):
        return tiles.reshape(AROUND // 2, ROWS, LINES)

    for pair in range(2):
        for k, layer in enumerate(layers):
            step = pair * LAYERS + k
            for copy in sums[step]:
                copy.wait_recv()
            if step + AHEAD < 2 * LAYERS:
                for i in (1, 2, 0):
                    sums[step + AHEAD][i].start()
            mine = own_part[x, pair, layer] + summands[0, pair, layer].astype(F32)
            theirs = summands[1, pair, layer].astype(F32) + summands[2, pair, layer].astype(F32)
            low, high = jnp.where(x == 0, mine, theirs), jnp.where(x == 0, theirs, mine)
            even, odd = regroup(rows(low), rows(high))
            tiles = jnp.stack([even, odd], axis=1).reshape(AROUND, ROWS, LINES)
            send1[pair, pl.ds(layer * AROUND, AROUND)] = tiles.astype(BF16)
            spread(send1, got1, pair, everyone[k], send_sem.at[0], recv1.at[pair])
        got1[pair, here] = send1[pair, here]

    for copy in small[2:]:
        copy.wait()
    for i in range(4):
        parts = []
        for k in range(3 * i, 3 * i + 3):
            top, column = TAPER_ROWS + k // 8 * LINES, k % 8 * LINES
            parts.append(packed[top : top + LINES, column : column + LINES].astype(F32))
        fine_v[i] = parts[0] + parts[1] + parts[2]
    turns = [packed[PACKED - 2 * LINES :, 2 * LINES * i : 2 * LINES * (i + 1)] for i in range(4)]
    passes = mask_v[pl.ds(me, 1), :].astype(F32) * (1.0 / LINES)
    cosine, sine = fine_v[2], fine_v[3]
    left = jnp.concatenate([cosine * passes, sine * passes], axis=1)
    right = jnp.concatenate(
        [jnp.concatenate([cosine, sine], axis=1), jnp.concatenate([sine, -cosine], axis=1)], axis=0
    )
    fan = jnp.dot(left, right, precision=lax.Precision.HIGHEST, preferred_element_type=F32)
    fan = jnp.concatenate(
        [fan, jnp.concatenate([-fan[:, LINES:], fan[:, :LINES]], axis=1)], axis=0
    )
    fan_high = fan.astype(BF16)
    fan_low = (fan - fan_high.astype(F32)).astype(BF16)

    twist_cos, twist_sin = fine_v[0], fine_v[1]

    def across_channels(pair):
        lines = lines_v.at[pair]
        lines[...] = got1[pair].astype(F32).reshape(PLANE * ROWS, LINES)

        def spot(half, imag, b):
            return pl.ds(half * ROWS // 2 + imag * PAIR + b, PLANE, stride=ROWS)

        picked = [
            [
                jnp.concatenate([lines[spot(h, imag, b), :] for h in range(2)], axis=0).astype(BF16)
                for b in range(PAIR)
            ]
            for imag in range(2)
        ]
        stacked = jnp.concatenate([jnp.concatenate(p, axis=1) for p in picked], axis=0)
        wave = jnp.dot(turns[0], stacked, preferred_element_type=F32)
        wave += jnp.dot(turns[1], stacked, preferred_element_type=F32)
        turned = []
        for b in range(PAIR):
            re = wave[:LINES, b * LINES : (b + 1) * LINES]
            im = wave[LINES:, b * LINES : (b + 1) * LINES]
            turned.append(
                jnp.concatenate(
                    [re * twist_cos + im * twist_sin, im * twist_cos - re * twist_sin], axis=1
                )
            )
        turned = jnp.concatenate(turned, axis=0)
        high = turned.astype(BF16)
        low = (turned - high.astype(F32)).astype(BF16)
        masked = jnp.dot(high, fan_high, preferred_element_type=F32)
        masked += jnp.dot(low, fan_high, preferred_element_type=F32)
        masked += jnp.dot(high, fan_low, preferred_element_type=F32)
        real, imag = [], []
        for b in range(PAIR):
            re = masked[b * LINES : (b + 1) * LINES, :LINES]
            im = masked[b * LINES : (b + 1) * LINES, LINES:]
            real.append(re * twist_cos - im * twist_sin)
            imag.append(im * twist_cos + re * twist_sin)
        straight = jnp.concatenate(
            [jnp.concatenate(real, axis=1), jnp.concatenate(imag, axis=1)], axis=0
        )
        high = straight.astype(BF16)
        low = (straight - high.astype(F32)).astype(BF16)
        back = jnp.dot(turns[2], high, preferred_element_type=F32)
        back += jnp.dot(turns[2], low, preferred_element_type=F32)
        back += jnp.dot(turns[3], high, preferred_element_type=F32)
        for h in range(2):
            for i in range(2):
                top = i * LINES + h * PLANE
                for b in range(PAIR):
                    lines[spot(h, i, b), :] = back[top : top + PLANE, b * LINES : (b + 1) * LINES]
        send2[pair] = lines[...].reshape(PLANE, ROWS, LINES).astype(BF16)

    rest = pl.ds(0, PLANE - 1)

    def transfer(ref, send, recv):
        return pltpu.make_async_remote_copy(
            ref, ref, send, recv, device_id=partner, device_id_type=MESH
        )

    for pair in range(2):
        transfer(got1.at[pair, rest], send_sem.at[0], recv1.at[pair]).wait_recv()
        across_channels(pair)
        for group in reversed(everyone):
            spread(send2, got2, pair, group, send_sem.at[1], recv2.at[pair, z])
        got2[pair, here] = send2[pair, here]

    for pair in range(2):
        for k, layer in reversed(list(enumerate(layers))):
            count = pl.ds(0, len(everyone[k]))
            transfer(got2.at[pair, count], send_sem.at[1], recv2.at[pair, layer]).wait_recv()
            tiles = got2[pair, pl.ds(layer * AROUND, AROUND)].astype(F32)
            tiles = tiles.reshape(AROUND // 2, 2, ROWS, LINES)
            low, high = regroup(tiles[:, 0], tiles[:, 1])
            split[0, pair, layer] = low.reshape(GROUP, LINES).astype(BF16)
            split[1, pair, layer] = high.reshape(GROUP, LINES).astype(BF16)
            for kind, half, peer in ((1, 1 - x, far), (2, 1 - x, diagonal), (0, x, partner)):
                pltpu.make_async_remote_copy(
                    split.at[half, pair, layer], passed.at[kind, pair, layer], pass_send,
                    pass_recv.at[kind, pair], device_id=peer, device_id_type=MESH,
                ).start()

    places = ((0, 0), (1, 1 + tm), (2, 2 - tm))

    def terms(block, half, pair, quarters):
        lines = block.astype(F32).reshape(BAND // 2, LINES).T.astype(BF16)
        rows = pl.ds(pl.multiple_of((2 * half + pair) * (BAND // 2), BAND // 2), BAND // 2)
        return [jnp.dot(lines, inv[i, rows, :], preferred_element_type=F32) for i in quarters]

    def arrived(kind, pair):
        transfer(passed.at[kind, pair], pass_send, pass_recv.at[kind, pair]).wait_recv()
        return passed[kind, pair]

    def put(column, value):
        out[:, pl.ds(column, QUARTER)] = (value * (1.0 / WINDOW)).astype(BF16)

    for copy in inv_copies:
        copy.wait()
    mine = [i for _, i in places]
    for k, term in enumerate(terms(split[x, 0], x, 0, mine)):
        frames[k] = term
    for k, term in enumerate(terms(split[x, 1], x, 1, mine)):
        frames[k] += term
    for k, term in enumerate(terms(arrived(1, 0), 1 - x, 0, mine)):
        frames[k] += term
    frames[2] += terms(arrived(2, 0), 1 - x, 0, [0])[0] + terms(arrived(0, 0), x, 0, [0])[0]
    last = terms(arrived(1, 1), 1 - x, 1, mine)
    put(outer, frames[0] + last[0])
    put(QUARTER, frames[1] + last[1])
    frames[2] += last[2]
    last = terms(arrived(2, 1), 1 - x, 1, [0])[0] + terms(arrived(0, 1), x, 1, [0])[0]
    put(shared, frames[2] + last)
    transfer(summands, sum_send, recv1.at[0]).wait_send()
    transfer(send1.at[:, rest], send_sem.at[0], recv1.at[0]).wait_send()
    transfer(send2.at[:, rest], send_sem.at[1], recv1.at[0]).wait_send()
    transfer(passed, pass_send, recv1.at[0]).wait_send()


def on_device(signal, fan_mask):
    far = pl.BlockSpec(memory_space=pltpu.HBM)
    block = (2, PLANE, ROWS, LINES)
    spectra = (2, LAYERS, GROUP, LINES)
    dma = pltpu.SemaphoreType.DMA
    vmem = pltpu.VMEM
    return pl.pallas_call(
        kernel,
        out_shape=jax.ShapeDtypeStruct(signal.shape, BF16),
        in_specs=[far] * 3,
        out_specs=pl.BlockSpec(memory_space=pltpu.VMEM),
        scratch_shapes=[
            vmem(signal.shape, BF16),
            vmem((LINES, LINES), jnp.int32),
            vmem((3, QUARTER, 2 * BAND), BF16),
            vmem((3, 2 * BAND, QUARTER), BF16),
            vmem((PACKED, 2 * BAND), BF16),
            vmem((16, QUARTER), F32),
            vmem((4, LINES, LINES), F32),
            vmem((2, *spectra), F32),
            vmem(spectra, BF16),
            vmem((2, *spectra), BF16),
            vmem((3, *spectra), BF16),
            vmem(block, BF16),
            vmem(block, BF16),
            vmem(block, BF16),
            vmem(block, BF16),
            vmem((2, *spectra), BF16),
            vmem((3, *spectra), BF16),
            vmem((2, PLANE * ROWS, LINES), F32),
            vmem((3, LINES, QUARTER), F32),
            dma((4,)),
            dma((6,)),
            dma(()),
            dma((2, 3, LAYERS)),
            dma((2,)),
            dma((2,)),
            dma((2, LAYERS)),
            dma(()),
            dma((3, 2)),
        ],
        compiler_params=pltpu.CompilerParams(
            collective_id=0, has_side_effects=True, vmem_limit_bytes=53 * 2**20
        ),
        cost_estimate=pl.CostEstimate(
            flops=5 * 10**9, bytes_accessed=20 * 10**6, transcendentals=0
        ),
    )(signal, fan_mask, tables())


def solution(mesh):
    return jax.shard_map(
        on_device,
        mesh=mesh,
        in_specs=(P("chan", "tm"), P()),
        out_specs=P("chan", "tm"),
        check_vma=False,
    )
```
